256 devices in a mesh: dp: 8 (over x, core), seg: 4 (over y), grp: 8 (over z).
Axes of the slice: x: 4, y: 4, z: 8, core: 2. Of those that a mesh axis runs over, the one named last changes fastest.
Arguments:
- query: bfloat16 [8, 4096, 2048], P('dp', ('seg', 'grp')), may hold values from -6 to 6
- key: bfloat16 [8, 4096, 2048], P('dp', ('seg', 'grp')), may hold values from -6 to 6
- value: bfloat16 [8, 4096, 2048], P('dp', ('seg', 'grp')), may hold values from -6 to 6
- dout: bfloat16 [8, 4096, 2048], P('dp', ('seg', 'grp')), may hold values from -0.125 to 0.125
- gate_in: bfloat16 [8, 4096, 16], P('dp', ('seg', 'grp'))
- gate_bias: float32 [16], replicated, may hold values from -1 to 1
- offsets: int32 [8, 4], P('dp'), may hold values from 0 to 4095, as said below
Outputs:
- query_grad: bfloat16 [8, 4096, 2048], P('dp', ('seg', 'grp'))
- key_grad: bfloat16 [8, 4096, 2048], P('dp', ('seg', 'grp'))
- value_grad: bfloat16 [8, 4096, 2048], P('dp', ('seg', 'grp'))
- gate_grad: bfloat16 [8, 4096, 16], P('dp', ('seg', 'grp'))
- bias_grad: float32 [16], replicated
The draws below stay inside these ranges and needn't reach their ends.
Inputs may be any that keep to these rules, and one draw needn't show every extreme that they name: `offsets`: each row holds 4 document starts in increasing order; the first is 0 and the last is 4095.
All inputs are finite; a program needn't handle non-finite values.
Results may differ from the reference program's by a relative error of at most 0.0045.
Values may be sent and summed in bfloat16 or wider, within the bound.
No kernel may reach another device: no remote copies, remote signals or barrier semaphores. Data moves between devices by JAX's collectives and lax.ppermute only.
A program may use at most 192 MiB of HBM per device.

```python
import math
import jax
import jax.numpy as jnp
from jax import lax

HEADS = 16
HEAD_DIM = 128
SPAN = 256
DOCS = 4
SEQS = 8
SEQUENCE_LENGTH = 4096
WIDTH = 2048


def draw_gate_in(key, part):
    key = jax.random.fold_in(key, 11)
    baseline_random_key, jitter_random_key, spike_random_key, boundary_random_key = jax.random.split(key, 4)
    array_shape = (SEQS, SEQUENCE_LENGTH, HEADS)
    baseline_level = jax.random.uniform(baseline_random_key, (SEQS, 1, HEADS), jnp.float32, math.log(0.5 / SEQUENCE_LENGTH), math.log(1.0 / 30.0))
    jitter_noise = jax.random.uniform(jitter_random_key, array_shape, jnp.float32, -0.8, 0.8)
    spike_values = jax.random.bernoulli(spike_random_key, 6.0 / SEQUENCE_LENGTH, array_shape)
    boundary_values = jax.random.uniform(boundary_random_key, array_shape, jnp.float32, -1.5, 0.0)
    return jnp.where(spike_values, boundary_values, baseline_level + jitter_noise).astype(jnp.bfloat16)


def one_row(row_key):
    shuffled = jax.random.permutation(row_key, SEQUENCE_LENGTH - 2) + 1
    inner_starts = jnp.sort(shuffled[:DOCS - 2]).astype(jnp.int32)
    return jnp.concatenate([jnp.zeros((1,), jnp.int32), inner_starts, jnp.full((1,), SEQUENCE_LENGTH - 1, jnp.int32)])


def draw_offsets(key, part):
    key = jax.random.fold_in(key, 5)
    row_keys = jax.random.split(key, SEQS)
    return jax.vmap(one_row)(row_keys)


def steps_of(stream_key, shape, cuts, smallest, largest):
    def one(dim, shards_of):
        heights = jax.random.uniform(jax.random.fold_in(jax.random.fold_in(stream_key, 6), dim), (shards_of,), jnp.float32, smallest / len(cuts), largest / len(cuts))
        return jnp.repeat(jnp.exp(heights), shape[dim] // shards_of).reshape((-1,) + (1,) * (len(shape) - dim - 1))

    loudness = one(*cuts[0])
    for cut in cuts[1:]:
        loudness = loudness * one(*cut)
    return loudness


def gaussian(rng, extent, scale, limit, shards=(), kind=jnp.bfloat16):
    drawn = scale * jax.random.normal(rng, extent, jnp.float32)
    if shards:
        drawn = drawn * steps_of(rng, extent, shards, -0.22, 0.18)
    return jnp.clip(drawn, -limit, limit).astype(kind)


def setup_inputs(seed: int = 0) -> dict:
    keys = jax.random.split(jax.random.key(seed), 8)
    query = gaussian(keys[0], (SEQS, SEQUENCE_LENGTH, WIDTH), 1.0, 6.0, ((0, 8), (1, 32)))
    key = gaussian(keys[1], (SEQS, SEQUENCE_LENGTH, WIDTH), 1.0, 6.0, ((0, 8), (1, 32)))
    value = gaussian(keys[2], (SEQS, SEQUENCE_LENGTH, WIDTH), 1.0, 6.0, ((0, 8), (1, 32)))
    dout = gaussian(keys[3], (SEQS, SEQUENCE_LENGTH, WIDTH), 0.02, 0.125, ((0, 8), (1, 32)))
    gate_in = draw_gate_in(jax.random.fold_in(keys[7], 71), 0)
    gate_bias = jnp.clip(jax.random.uniform(keys[5], (HEADS,), jnp.float32, -1.0, 1.0), -1.0, 1.0)
    offsets = draw_offsets(jax.random.fold_in(keys[7], 71), 0)
    return {"query": query, "key": key, "value": value, "dout": dout, "gate_in": gate_in, "gate_bias": gate_bias, "offsets": offsets}


def forward(query_full, key_full, value_full, log_decay, doc_ids, before, state_in):
    length_here = query_full.shape[0]
    span_len = min(SPAN, length_here)
    span_count = length_here // span_len
    highest = lax.Precision.HIGHEST
    scaled = query_full * HEAD_DIM ** (-0.5)

    def shaped(array):
        return array.reshape((span_count, span_len) + array.shape[1:])
    prior_docs = jnp.concatenate([before.reshape(1), doc_ids[:-1]]).reshape(span_count, span_len)[:, 0]
    within = jnp.arange(span_len, dtype=jnp.int32)
    causal = within[:, None] >= within[None, :]

    def advance(carry_state, pieces):
        query_blk, key_blk, value_blk, decay_blk, doc_blk, prior_doc = pieces
        cumulative = jnp.cumsum(decay_blk, axis=0)
        carried = (doc_blk == prior_doc).astype(jnp.float32)
        linked = causal & (doc_blk[:, None] == doc_blk[None, :])
        difference = cumulative.T[:, :, None] - cumulative.T[:, None, :]
        weights = jnp.exp(jnp.where(linked[None], difference, 0.0)) * linked[None].astype(jnp.float32)
        scores = jnp.einsum('ihd,jhd->hij', query_blk, key_blk, precision=highest) * weights
        intra_part = jnp.einsum('hij,jhd->ihd', scores, value_blk, precision=highest)
        entry_decay = jnp.exp(cumulative) * carried[:, None]
        inter_part = jnp.einsum('ihd,hde->ihe', query_blk * entry_decay[:, :, None], carry_state, precision=highest)
        last_total = cumulative[-1]
        tail_decay = jnp.exp(last_total[None, :] - cumulative) * (doc_blk == doc_blk[-1]).astype(jnp.float32)[:, None]
        state_next = (carried[-1] * jnp.exp(last_total))[:, None, None] * carry_state + jnp.einsum('jhd,jhe->hde', key_blk * tail_decay[:, :, None], value_blk, precision=highest)
        return (state_next, intra_part + inter_part)
    state_out, outputs = lax.scan(advance, state_in, (shaped(scaled), shaped(key_full), shaped(value_full), shaped(log_decay), shaped(doc_ids), prior_docs))
    return (outputs.reshape(query_full.shape), state_out)

def one_sequence(pieces, gate_bias):
    query_row, key_row, value_row, dout_row, gate_row, offset_row = pieces
    positions = jnp.arange(SEQUENCE_LENGTH, dtype=jnp.int32)
    doc_ids = lax.optimization_barrier(jnp.sum((offset_row[None, :] <= positions[:, None]).astype(jnp.int32), axis=1))
    before = jnp.asarray(-1, jnp.int32)
    state_zero = jnp.zeros((HEADS, HEAD_DIM, HEAD_DIM), jnp.float32)

    def widen(array):
        return array.astype(jnp.float32).reshape(SEQUENCE_LENGTH, HEADS, HEAD_DIM)
    logits = gate_row.astype(jnp.float32) + gate_bias[None, :]

    def layer(query_arg, key_arg, value_arg, logit_arg):
        return forward(query_arg, key_arg, value_arg, -jax.nn.softplus(logit_arg), doc_ids, before, state_zero)
    primal, pullback = jax.vjp(layer, widen(query_row), widen(key_row), widen(value_row), logits)
    query_back, key_back, value_back, logit_back = pullback((widen(dout_row), jnp.zeros_like(primal[1])))

    def narrow(array):
        return array.reshape(SEQUENCE_LENGTH, WIDTH).astype(jnp.bfloat16)
    return (narrow(query_back), narrow(key_back), narrow(value_back), logit_back.astype(jnp.bfloat16), lax.optimization_barrier(jnp.sum(logit_back, axis=0)))

def reference(query, key, value, dout, gate_in, gate_bias, offsets):
    results = lax.map(lambda pieces: one_sequence(pieces, gate_bias), (query, key, value, dout, gate_in, offsets))
    return (results[0], results[1], results[2], results[3], lax.optimization_barrier(jnp.sum(results[4], axis=0)))
```

```python
import jax
import jax.numpy as jnp
from jax import lax
from jax.experimental import pallas as pl
from jax.experimental.pallas import tpu as pltpu
from jax.sharding import PartitionSpec as P

HEAD_DIM = 128
SCALE = HEAD_DIM ** (-0.5)
DOCS = 4
LINE = ("seg", "grp")
ALL = ("dp", "seg", "grp")
TAIL = 16
F32 = jnp.float32
BF16 = jnp.bfloat16
VMEM = pl.BlockSpec(memory_space=pltpu.VMEM)
SMEM = pl.BlockSpec(memory_space=pltpu.SMEM)
HIGHEST = lax.Precision.HIGHEST


def nn(a, b, precision=None):
    return lax.dot_general(
        a, b, (((1,), (0,)), ((), ())), precision=precision, preferred_element_type=F32
    )


def nt(a, b, precision=None):
    return lax.dot_general(
        a, b, (((1,), (1,)), ((), ())), precision=precision, preferred_element_type=F32
    )


def tn(a, b, precision=None):
    return lax.dot_general(
        a, b, (((0,), (0,)), ((), ())), precision=precision, preferred_element_type=F32
    )


def split2(x):
    hi = x.astype(BF16)
    return hi, (x - hi.astype(F32)).astype(BF16)


def encode(x):
    top = jnp.maximum(jnp.max(jnp.abs(x), axis=0, keepdims=True), 1e-30)
    power = jnp.ceil(jnp.log2(top))
    steps = jnp.clip(jnp.floor(x * jnp.exp2(15.0 - power) + 0.5), -32767.0, 32767.0)
    return whole16(steps), power


def whole16(x):
    return x.astype(jnp.int32).astype(jnp.int16)


def wide(x):
    return x.astype(jnp.int32).astype(F32)


def rows16(*rows):
    at = lax.broadcasted_iota(jnp.int32, (TAIL, HEAD_DIM), 0)
    total = jnp.zeros((TAIL, HEAD_DIM), F32)
    for i, row in enumerate(rows):
        total = jnp.where(at == i, row, total)
    return whole16(total)


def doc_of(pos, offsets_ref):
    total = (pos >= offsets_ref[0, 0]).astype(jnp.int32)
    for i in range(1, DOCS):
        total = total + (pos >= offsets_ref[0, i]).astype(jnp.int32)
    return total


def decays(gate_ref, bias_ref, offsets_ref):
    length = gate_ref.shape[1]
    first = (lax.axis_index("seg") * lax.axis_size("grp") + lax.axis_index("grp")) * length
    logits = gate_ref[0].astype(F32) + bias_ref[...]
    step = -(jnp.maximum(logits, 0.0) + jnp.log1p(jnp.exp(-jnp.abs(logits))))
    rows = lax.broadcasted_iota(jnp.int32, (length, length), 0)
    cols = lax.broadcasted_iota(jnp.int32, (length, length), 1)
    causal = rows >= cols
    cumulative = nn(causal.astype(F32), step, HIGHEST)
    doc = doc_of(first + lax.broadcasted_iota(jnp.int32, (length, 1), 0), offsets_ref)
    doc_last = doc_of(first + length - 1, offsets_ref)
    before = jnp.where(first > 0, doc_of(first - 1, offsets_ref), -1)
    last_total = cumulative[length - 1 :, :]
    entry = jnp.exp(cumulative) * (doc == before).astype(F32)
    tail = jnp.exp(last_total - cumulative) * (doc == doc_last).astype(F32)
    through = jnp.where(doc_last == before, jnp.maximum(last_total, -120.0), -128.0)
    return first, logits, step, causal, cumulative, doc, entry, tail, through


def states_kernel(query_ref, key_ref, value_ref, dout_ref, gate_ref, bias_ref, offsets_ref, pay_ref):
    heads = bias_ref.shape[1]
    _, _, _, _, _, _, entry, tail, through = decays(gate_ref, bias_ref, offsets_ref)
    coarse = jnp.floor(through * 256.0 + 0.5)
    fine = jnp.floor((through - coarse / 256.0) * 8388608.0 + 0.5)
    for h in range(heads):
        cols = pl.ds(h * HEAD_DIM, HEAD_DIM)
        one = slice(h, h + 1)
        for slot, left_ref, right_ref, weight in (
            (2 * h, key_ref, value_ref, tail[:, one]),
            (2 * h + 1, query_ref, dout_ref, entry[:, one] * SCALE),
        ):
            upper, lower = split2(left_ref[0, :, cols].astype(F32) * weight)
            right = right_ref[0, :, cols]
            steps, power = encode(tn(upper, right) + tn(lower, right))
            pay_ref[slot, 0:HEAD_DIM, :] = steps
            pay_ref[slot, HEAD_DIM : HEAD_DIM + TAIL, :] = rows16(power, coarse[:, one], fine[:, one])


def scan_kernel(pay_ref, out_ref):
    count = pay_ref.shape[0]
    mine = lax.axis_index("seg") * lax.axis_size("grp") + lax.axis_index("grp")
    backward = lax.rem(mine, 2) == 1

    def turn(step, carry):
        chunk = jnp.where(backward, count - 1 - step, step)
        steps, power = encode(carry)
        out_ref[chunk, 0:HEAD_DIM, :] = steps
        out_ref[chunk, HEAD_DIM : HEAD_DIM + TAIL, :] = rows16(power)
        tail = wide(pay_ref[chunk, HEAD_DIM : HEAD_DIM + TAIL, :])
        passing = jnp.exp(tail[1:2] / 256.0 + tail[2:3] / 8388608.0)
        own = wide(pay_ref[chunk, 0:HEAD_DIM, :]) * jnp.exp2(tail[0:1] - 15.0)
        return passing * carry + own

    lax.fori_loop(0, count, turn, jnp.zeros((HEAD_DIM, HEAD_DIM), F32), unroll=4)


def grads_kernel(
    query_ref, key_ref, value_ref, dout_ref, gate_ref, bias_ref, offsets_ref, state_ref,
    dq_ref, dk_ref, dv_ref, dgate_ref, dbias_ref,
):
    length = gate_ref.shape[1]
    heads = bias_ref.shape[1]
    first, logits, step, causal, cumulative, doc, entry, tail, through = decays(
        gate_ref, bias_ref, offsets_ref
    )
    cumulative_row = lax.dot_general(
        step, causal.astype(F32), (((0,), (1,)), ((), ())), precision=HIGHEST, preferred_element_type=F32
    )
    doc_row = doc_of(first + lax.broadcasted_iota(jnp.int32, (1, length), 1), offsets_ref)
    linked = causal & (doc == doc_row)
    lane = lax.broadcasted_iota(jnp.int32, (length, heads), 1)
    sublane = lax.broadcasted_iota(jnp.int32, (heads, length), 0)
    ends = jnp.zeros((length, heads), F32)
    starts = jnp.zeros((length, heads), F32)
    ends_row = jnp.zeros((heads, length), F32)
    whole = jnp.zeros((1, heads), F32)
    for h in range(heads):
        cols = pl.ds(h * HEAD_DIM, HEAD_DIM)
        one = slice(h, h + 1)
        q, k, v, d = (ref[0, :, cols] for ref in (query_ref, key_ref, value_ref, dout_ref))
        q32, k32 = q.astype(F32), k.astype(F32)
        state32, grad32 = (
            wide(state_ref[slot, 0:HEAD_DIM, :])
            * jnp.exp2(wide(state_ref[slot, HEAD_DIM : HEAD_DIM + TAIL, :])[0:1] - 15.0)
            for slot in (2 * h, 2 * h + 1)
        )
        state, state_low = split2(state32)
        grad, grad_low = split2(grad32)
        weights = jnp.where(
            linked, jnp.exp(jnp.where(linked, cumulative[:, one] - cumulative_row[one, :], 0.0)), 0.0
        ) * SCALE
        probs = nt(q, k) * weights
        dprobs = nt(d, v)
        pairs = probs * dprobs
        probs = probs.astype(BF16)
        dscores = (dprobs * weights).astype(BF16)
        dq_inter = (entry[:, one] * SCALE) * (nt(d, state) + nt(d, state_low))
        dk_inter = tail[:, one] * (nt(v, grad) + nt(v, grad_low))
        dq_ref[0, :, cols] = (nn(dscores, k) + dq_inter).astype(BF16)
        dk_ref[0, :, cols] = (tn(dscores, q) + dk_inter).astype(BF16)
        dv_ref[0, :, cols] = (tn(probs, d) + tail[:, one] * nn(k, grad)).astype(BF16)
        at_end = jnp.sum(pairs + q32 * dq_inter, axis=1, keepdims=True)
        at_start = jnp.sum(k32 * dk_inter, axis=1, keepdims=True)
        product = jnp.sum(state32 * grad32, keepdims=True)
        ends = jnp.where(lane == h, at_end, ends)
        starts = jnp.where(lane == h, at_start, starts)
        ends_row = jnp.where(sublane == h, jnp.sum(pairs, axis=0, keepdims=True), ends_row)
        whole = jnp.where(lane[0:1] == h, product, whole)
    causal = causal.astype(F32)
    after = tn(causal, ends, HIGHEST) - lax.dot_general(
        causal, ends_row, (((0,), (1,)), ((), ())), precision=HIGHEST, preferred_element_type=F32
    )
    earlier = nn(causal, starts, HIGHEST) - starts
    dstep = after + earlier + jnp.exp(through) * whole
    dlogit = -dstep / (1.0 + jnp.exp(-logits))
    dgate_ref[0] = dlogit.astype(BF16)
    dbias_ref[...] = jnp.sum(dlogit, axis=0, keepdims=True)


PARAMS = pltpu.CompilerParams(vmem_limit_bytes=48 * 1024 * 1024)


def shards(query, key, value, dout, gate_in, gate_bias, offsets):
    heads = gate_bias.shape[0]
    count = lax.axis_size("seg") * lax.axis_size("grp")
    bias_row = gate_bias.reshape(1, heads)
    inputs = (query, key, value, dout, gate_in, bias_row, offsets)
    specs = [VMEM] * 6 + [SMEM]
    pay = pl.pallas_call(
        states_kernel,
        out_shape=jax.ShapeDtypeStruct((2 * heads, HEAD_DIM + TAIL, HEAD_DIM), jnp.int16),
        in_specs=specs,
        out_specs=VMEM,
        compiler_params=PARAMS,
    )(*inputs)
    pay = lax.all_to_all(pay, LINE, split_axis=0, concat_axis=0, tiled=True)
    carried = pl.pallas_call(
        scan_kernel,
        out_shape=jax.ShapeDtypeStruct((count, HEAD_DIM + TAIL, HEAD_DIM), jnp.int16),
        in_specs=[VMEM],
        out_specs=VMEM,
        compiler_params=PARAMS,
    )(pay)
    carried = lax.all_to_all(carried, LINE, split_axis=0, concat_axis=0, tiled=True)
    like = jax.ShapeDtypeStruct(query.shape, BF16)
    dq, dk, dv, dgate, dbias = pl.pallas_call(
        grads_kernel,
        out_shape=(
            like,
            like,
            like,
            jax.ShapeDtypeStruct(gate_in.shape, BF16),
            jax.ShapeDtypeStruct((1, heads), F32),
        ),
        in_specs=specs + [VMEM],
        out_specs=(VMEM,) * 5,
        compiler_params=PARAMS,
    )(*inputs, carried)
    everywhere = lax.all_to_all(
        jnp.broadcast_to(dbias[None], (lax.axis_size(ALL), 1, heads)), ALL, split_axis=0, concat_axis=0, tiled=True
    )
    return dq, dk, dv, dgate, jnp.sum(everywhere, axis=(0, 1))


def solution(mesh):
    rows = P("dp", LINE, None)
    return jax.shard_map(
        shards,
        mesh=mesh,
        in_specs=(rows, rows, rows, rows, rows, P(), P("dp", None)),
        out_specs=(rows, rows, rows, rows, P()),
        check_vma=False,
    )
```

```python
import jax
import jax.numpy as jnp
from jax import lax
from jax.experimental import pallas as pl
from jax.experimental.pallas import tpu as pltpu
from jax.sharding import PartitionSpec as P

HEAD_DIM = 128
SCALE = HEAD_DIM ** (-0.5)
DOCS = 4
LINE = ("seg", "grp")
ALL = ("dp", "seg", "grp")
TAIL = 16
LANES = 128
F32 = jnp.float32
BF16 = jnp.bfloat16
I16 = jnp.int16
VMEM = pl.BlockSpec(memory_space=pltpu.VMEM)
SMEM = pl.BlockSpec(memory_space=pltpu.SMEM)
HBM = pl.BlockSpec(memory_space=pl.ANY)
HIGHEST = lax.Precision.HIGHEST
PARAMS = pltpu.CompilerParams(vmem_limit_bytes=48 * 1024 * 1024)


def dot(a, b, over, precision=None):
    return lax.dot_general(
        a, b, (((over[0],), (over[1],)), ((), ())), precision=precision, preferred_element_type=F32
    )


def nn(a, b, precision=None):
    return dot(a, b, (1, 0), precision)


def nt(a, b, precision=None):
    return dot(a, b, (1, 1), precision)


def tn(a, b, precision=None):
    return dot(a, b, (0, 0), precision)


def split2(x):
    hi = x.astype(BF16)
    return hi, (x - hi.astype(F32)).astype(BF16)


def matrix(m):
    return pl.ds(m * HEAD_DIM, HEAD_DIM)


def tail_of(ref):
    return pl.ds(ref.shape[-2] - TAIL, TAIL)


def encode(x):
    top = jnp.maximum(jnp.max(jnp.abs(x), axis=0, keepdims=True), 1e-30)
    power = jnp.ceil(jnp.log2(top))
    return jnp.clip(jnp.floor(x * jnp.exp2(15.0 - power) + 0.5), -32767.0, 32767.0), power


def decode(steps, power):
    return wide(steps) * jnp.exp2(power - 15.0)


def log_parts(log):
    log = jnp.maximum(log, -128.0)
    coarse = jnp.floor(log * 256.0 + 0.5)
    return coarse, jnp.floor((log - coarse / 256.0) * 8388608.0 + 0.5)


def log_whole(coarse, fine):
    return coarse / 256.0 + fine / 8388608.0


def whole16(x):
    return x.astype(jnp.int32).astype(I16)


def wide(x):
    return x.astype(jnp.int32).astype(F32)


def rows16(*rows):
    at = lax.broadcasted_iota(jnp.int32, (TAIL, LANES), 0)
    total = jnp.zeros((TAIL, LANES), F32)
    for i, row in enumerate(rows):
        total = jnp.where(at == i, row, total)
    return whole16(total)


def iota(shape, dim):
    return lax.broadcasted_iota(jnp.int32, shape, dim)


def doc_of(pos, offsets_ref):
    total = (pos >= offsets_ref[0, 0]).astype(jnp.int32)
    for i in range(1, DOCS):
        total = total + (pos >= offsets_ref[0, i]).astype(jnp.int32)
    return total


def decays(gate_ref, bias_ref, offsets_ref):
    heads, length = gate_ref.shape[1:]
    first = (lax.axis_index("seg") * lax.axis_size("grp") + lax.axis_index("grp")) * length
    same = iota((heads, heads), 0) == iota((heads, heads), 1)
    bias = jnp.sum(jnp.where(same, bias_ref[...], 0.0), axis=1, keepdims=True)
    logits = gate_ref[0].astype(F32) + bias
    step = -(jnp.maximum(logits, 0.0) + jnp.log1p(jnp.exp(-jnp.abs(logits))))
    causal = iota((length, length), 0) >= iota((length, length), 1)
    cumulative = nt(causal.astype(F32), step, HIGHEST)
    doc = doc_of(first + iota((length, 1), 0), offsets_ref)
    doc_last = doc_of(first + length - 1, offsets_ref)
    before = jnp.where(first > 0, doc_of(first - 1, offsets_ref), -1)
    last_total = cumulative[length - 1 :, :]
    entry = jnp.exp(cumulative) * (doc == before).astype(F32)
    tail = jnp.exp(last_total - cumulative) * (doc == doc_last).astype(F32)
    passes = doc_last == before
    return first, logits, step, causal, cumulative, doc, entry, tail, passes


def states_kernel(
    query_ref, key_ref, value_ref, dout_ref, gate_ref, bias_ref, offsets_ref, pay_ref, held, sems
):
    heads = bias_ref.shape[1]
    parts = sems.shape[1]
    width = query_ref.shape[2] // parts
    copies = [
        [
            pltpu.make_async_copy(
                ref.at[0, :, pl.ds(p * width, width)], held.at[i, :, pl.ds(p * width, width)], sems.at[i, p]
            )
            for i, ref in enumerate((query_ref, key_ref, value_ref, dout_ref))
        ]
        for p in range(parts)
    ]
    for group in copies:
        for copy in group:
            copy.start()
    _, _, _, _, cumulative, _, entry, tail, passes = decays(gate_ref, bias_ref, offsets_ref)
    coarse, fine = log_parts(jnp.where(passes, jnp.maximum(cumulative[-1:, :], -120.0), -128.0))
    powers = {}
    for h in range(heads):
        if h % (heads // parts) == 0:
            for copy in copies[h // (heads // parts)]:
                copy.wait()
        cols = matrix(h)
        one = slice(h, h + 1)
        slot, m = divmod(h, 2)
        for place, left, right, weight in (
            (m, 1, 2, tail[:, one]),
            (2 + m, 0, 3, entry[:, one] * SCALE),
        ):
            upper, lower = split2(held[left, :, cols].astype(F32) * weight)
            right = held[right, :, cols]
            steps, powers[place] = encode(tn(upper, right) + tn(lower, right))
            pay_ref[slot, matrix(place), :] = whole16(steps)
        if m == 1:
            pay_ref[slot, tail_of(pay_ref), :] = rows16(
                *(powers[i] for i in range(4)),
                *(x[:, i : i + 1] for i in (h - 1, h) for x in (coarse, fine)),
            )


def totals_kernel(pay_ref, *send_refs):
    count = pay_ref.shape[0]
    tails = [wide(pay_ref[c, tail_of(pay_ref), :]) for c in range(count)]
    mine, segments = lax.axis_index("seg"), lax.axis_size("seg")
    ends, logs = [], []
    for m in range(2):
        log = [log_whole(t[4 + 2 * m : 5 + 2 * m], t[5 + 2 * m : 6 + 2 * m]) for t in tails]
        for place, order in ((m, range(count)), (2 + m, range(count - 1, -1, -1))):
            carry = jnp.zeros((HEAD_DIM, HEAD_DIM), F32)
            for c in order:
                carry = jnp.exp(log[c]) * carry + decode(
                    pay_ref[c, matrix(place), :], tails[c][place : place + 1]
                )
            ends.append(encode(carry))
        logs.extend(log_parts(sum(log)))
    for distance, send_ref in enumerate(send_refs, 1):
        later = mine + distance < segments
        for m in range(2):
            send_ref[matrix(m), :] = whole16(jnp.where(later, ends[2 * m][0], ends[2 * m + 1][0]))
        send_ref[tail_of(send_ref), :] = rows16(
            *(jnp.where(later, ends[2 * m][1], ends[2 * m + 1][1]) for m in range(2)), *logs
        )


def scan_kernel(pay_ref, *refs):
    *got_refs, out_ref = refs
    count = pay_ref.shape[0]
    mine = lax.axis_index("seg")
    tails = [wide(pay_ref[c, tail_of(pay_ref), :]) for c in range(count)]
    got_tails = [wide(ref[tail_of(ref), :]) for ref in got_refs]
    powers = [[None] * 4 for _ in range(count)]
    for m in range(2):
        log = [log_whole(t[4 + 2 * m : 5 + 2 * m], t[5 + 2 * m : 6 + 2 * m]) for t in tails]
        sent = [
            (jnp.exp(log_whole(t[2 + 2 * m : 3 + 2 * m], t[3 + 2 * m : 4 + 2 * m])), decode(ref[matrix(m), :], t[m : m + 1]))
            for ref, t in zip(got_refs, got_tails)
        ]
        state = jnp.zeros((HEAD_DIM, HEAD_DIM), F32)
        for d in range(len(sent), 0, -1):
            state = jnp.where(mine >= d, sent[d - 1][0] * state + sent[d - 1][1], state)
        grad = jnp.zeros((HEAD_DIM, HEAD_DIM), F32)
        for d in range(1, len(sent) + 1):
            grad = jnp.where(mine < d, sent[d - 1][0] * grad + sent[d - 1][1], grad)
        for place, carry, order in ((m, state, range(count)), (2 + m, grad, range(count - 1, -1, -1))):
            for i, c in enumerate(order):
                steps, powers[c][place] = encode(carry)
                out_ref[c, matrix(place), :] = whole16(steps)
                if i < count - 1:
                    carry = jnp.exp(log[c]) * carry + decode(
                        pay_ref[c, matrix(place), :], tails[c][place : place + 1]
                    )
    for c in range(count):
        out_ref[c, tail_of(out_ref), :] = rows16(*powers[c])


def grads_kernel(
    query_ref, key_ref, value_ref, dout_ref, gate_ref, bias_ref, offsets_ref, state_ref,
    dq_ref, dk_ref, dv_ref, dgate_ref, dbias_ref,
):
    heads, length = gate_ref.shape[1:]
    first, logits, step, causal, cumulative, doc, entry, tail, passes = decays(
        gate_ref, bias_ref, offsets_ref
    )
    cumulative_row = nt(step, causal.astype(F32), HIGHEST)
    linked = causal & (doc == doc_of(first + iota((1, length), 1), offsets_ref))
    lane = iota((length, heads), 1)
    sublane = iota((heads, length), 0)
    ends = jnp.zeros((length, heads), F32)
    starts = jnp.zeros((length, heads), F32)
    ends_row = jnp.zeros((heads, length), F32)
    whole = jnp.zeros((heads, 1), F32)
    for h in range(heads):
        cols = matrix(h)
        one = slice(h, h + 1)
        q, k, v, d = (ref[0, :, cols] for ref in (query_ref, key_ref, value_ref, dout_ref))
        q32, k32 = q.astype(F32), k.astype(F32)
        slot, m = divmod(h, 2)
        powers = wide(state_ref[slot, tail_of(state_ref), :])
        state32, grad32 = (
            decode(state_ref[slot, matrix(place), :], powers[place : place + 1]) for place in (m, 2 + m)
        )
        state, state_low = split2(state32)
        grad, grad_low = split2(grad32)
        weights = jnp.where(
            linked, jnp.exp(jnp.where(linked, cumulative[:, one] - cumulative_row[one, :], 0.0)), 0.0
        ) * SCALE
        probs = nt(q, k) * weights
        dprobs = nt(d, v)
        pairs = probs * dprobs
        probs = probs.astype(BF16)
        dscores = (dprobs * weights).astype(BF16)
        dq_inter = (entry[:, one] * SCALE) * (nt(d, state) + nt(d, state_low))
        dk_inter = tail[:, one] * (nt(v, grad) + nt(v, grad_low))
        dq_ref[0, :, cols] = (nn(dscores, k) + dq_inter).astype(BF16)
        dk_ref[0, :, cols] = (tn(dscores, q) + dk_inter).astype(BF16)
        dv_ref[0, :, cols] = (tn(probs, d) + tail[:, one] * nn(k, grad)).astype(BF16)
        at_end = jnp.sum(pairs + q32 * dq_inter, axis=1, keepdims=True)
        at_start = jnp.sum(k32 * dk_inter, axis=1, keepdims=True)
        product = jnp.sum(state32 * grad32, keepdims=True)
        ends = jnp.where(lane == h, at_end, ends)
        starts = jnp.where(lane == h, at_start, starts)
        ends_row = jnp.where(sublane == h, jnp.sum(pairs, axis=0, keepdims=True), ends_row)
        whole = jnp.where(sublane[:, :1] == h, product, whole)
    through = jnp.where(passes, jnp.exp(cumulative_row[:, length - 1 :]), 0.0)
    causal = causal.astype(F32)
    earlier = (iota((length, length), 0) < iota((length, length), 1)).astype(F32)
    dstep = (
        tn(ends, causal, HIGHEST)
        - nn(ends_row, causal, HIGHEST)
        + tn(starts, earlier, HIGHEST)
        + through * whole
    )
    dlogit = -dstep / (1.0 + jnp.exp(-logits))
    dgate_ref[0] = dlogit.astype(BF16)
    same = iota((heads, heads), 0) == iota((heads, heads), 1)
    dbias_ref[...] = jnp.sum(
        jnp.where(same, jnp.sum(dlogit, axis=1, keepdims=True), 0.0), axis=0, keepdims=True
    )


def call(kernel, out_shape, in_specs, **more):
    several = isinstance(out_shape, tuple)
    return pl.pallas_call(
        kernel,
        out_shape=out_shape,
        in_specs=in_specs,
        out_specs=(VMEM,) * len(out_shape) if several else VMEM,
        compiler_params=PARAMS,
        **more,
    )


def shards(query, key, value, dout, gate_in, gate_bias, offsets):
    heads = gate_bias.shape[0]
    count, segments = lax.axis_size("grp"), lax.axis_size("seg")
    gates = jnp.swapaxes(gate_in, 1, 2)
    rest = (gates, gate_bias.reshape(1, heads), offsets)
    packed = jax.ShapeDtypeStruct((count, 4 * HEAD_DIM + TAIL, LANES), I16)
    pay = call(
        states_kernel,
        packed,
        [HBM] * 4 + [VMEM] * 2 + [SMEM],
        scratch_shapes=[pltpu.VMEM((4,) + query.shape[1:], BF16), pltpu.SemaphoreType.DMA((4, 4))],
    )(query, key, value, dout, *rest)
    pay = lax.all_to_all(pay, "grp", split_axis=0, concat_axis=0, tiled=True)
    total = jax.ShapeDtypeStruct((2 * HEAD_DIM + TAIL, LANES), I16)
    sends = call(totals_kernel, (total,) * (segments - 1), [VMEM])(pay)
    got = [
        lax.ppermute(send, "seg", [(i, (i + d) % segments) for i in range(segments)])
        for d, send in enumerate(sends, 1)
    ]
    carried = call(scan_kernel, packed, [VMEM] * segments)(pay, *got)
    carried = lax.all_to_all(carried, "grp", split_axis=0, concat_axis=0, tiled=True)
    like = jax.ShapeDtypeStruct(query.shape, BF16)
    dq, dk, dv, dgate, dbias = call(
        grads_kernel,
        (
            like,
            like,
            like,
            jax.ShapeDtypeStruct(gates.shape, BF16),
            jax.ShapeDtypeStruct((1, heads), F32),
        ),
        [VMEM] * 6 + [SMEM, VMEM],
    )(query, key, value, dout, *rest, carried)
    everywhere = lax.all_to_all(
        jnp.broadcast_to(dbias[None], (lax.axis_size(ALL), 1, heads)), ALL, split_axis=0, concat_axis=0, tiled=True
    )
    return dq, dk, dv, jnp.swapaxes(dgate, 1, 2), jnp.sum(everywhere, axis=(0, 1))


def solution(mesh):
    rows = P("dp", LINE, None)
    return jax.shard_map(
        shards,
        mesh=mesh,
        in_specs=(rows, rows, rows, rows, rows, P(), P("dp", None)),
        out_specs=(rows, rows, rows, rows, P()),
        check_vma=False,
    )
```

```python
import jax
import jax.numpy as jnp
from jax import lax
from jax.experimental import pallas as pl
from jax.experimental.pallas import tpu as pltpu
from jax.sharding import PartitionSpec as P

HEAD_DIM = 128
SCALE = HEAD_DIM ** (-0.5)
DOCS = 4
LINE = ("seg", "grp")
ALL = ("dp", "seg", "grp")
TAIL = 16
LANES = 128
F32 = jnp.float32
BF16 = jnp.bfloat16
I16 = jnp.int16
VMEM = pl.BlockSpec(memory_space=pltpu.VMEM)
SMEM = pl.BlockSpec(memory_space=pltpu.SMEM)
HBM = pl.BlockSpec(memory_space=pltpu.HBM)
HIGHEST = lax.Precision.HIGHEST
PARAMS = pltpu.CompilerParams(vmem_limit_bytes=20 * 1024 * 1024)


def dot(a, b, over, precision=None):
    return lax.dot_general(
        a, b, (((over[0],), (over[1],)), ((), ())), precision=precision, preferred_element_type=F32
    )


def nn(a, b, precision=None):
    return dot(a, b, (1, 0), precision)


def nt(a, b, precision=None):
    return dot(a, b, (1, 1), precision)


def tn(a, b, precision=None):
    return dot(a, b, (0, 0), precision)


def split2(x):
    hi = x.astype(BF16)
    return hi, (x - hi.astype(F32)).astype(BF16)


def matrix(m):
    return pl.ds(m * HEAD_DIM, HEAD_DIM)


def tail_of(ref):
    return pl.ds(ref.shape[-2] - TAIL, TAIL)


def encode(x):
    top = jnp.maximum(jnp.max(jnp.abs(x), axis=0, keepdims=True), 1e-30)
    power = jnp.ceil(jnp.log2(top))
    return jnp.clip(jnp.floor(x * jnp.exp2(15.0 - power) + 0.5), -32767.0, 32767.0), power


def decode(steps, power):
    return wide(steps) * jnp.exp2(power - 15.0)


def log_parts(log):
    log = jnp.maximum(log, -128.0)
    coarse = jnp.floor(log * 256.0 + 0.5)
    return coarse, jnp.floor((log - coarse / 256.0) * 8388608.0 + 0.5)


def log_whole(coarse, fine):
    return coarse / 256.0 + fine / 8388608.0


def whole16(x):
    return x.astype(jnp.int32).astype(I16)


def wide(x):
    return x.astype(jnp.int32).astype(F32)


def rows16(*rows):
    at = lax.broadcasted_iota(jnp.int32, (TAIL, LANES), 0)
    total = jnp.zeros((TAIL, LANES), F32)
    for i, row in enumerate(rows):
        total = jnp.where(at == i, row, total)
    return whole16(total)


def iota(shape, dim):
    return lax.broadcasted_iota(jnp.int32, shape, dim)


def doc_of(pos, offsets_ref):
    total = (pos >= offsets_ref[0, 0]).astype(jnp.int32)
    for i in range(1, DOCS):
        total = total + (pos >= offsets_ref[0, i]).astype(jnp.int32)
    return total


def decays(gate_ref, bias_ref, offsets_ref):
    heads, length = gate_ref.shape[1:]
    first = (lax.axis_index("seg") * lax.axis_size("grp") + lax.axis_index("grp")) * length
    same = iota((heads, heads), 0) == iota((heads, heads), 1)
    bias = jnp.sum(jnp.where(same, bias_ref[...], 0.0), axis=1, keepdims=True)
    logits = gate_ref[0].astype(F32) + bias
    step = -(jnp.maximum(logits, 0.0) + jnp.log1p(jnp.exp(-jnp.abs(logits))))
    causal = iota((length, length), 0) >= iota((length, length), 1)
    cumulative = nt(causal.astype(F32), step, HIGHEST)
    doc = doc_of(first + iota((length, 1), 0), offsets_ref)
    doc_last = doc_of(first + length - 1, offsets_ref)
    before = jnp.where(first > 0, doc_of(first - 1, offsets_ref), -1)
    last_total = cumulative[length - 1 :, :]
    entry = jnp.exp(cumulative) * (doc == before).astype(F32)
    tail = jnp.exp(last_total - cumulative) * (doc == doc_last).astype(F32)
    passes = doc_last == before
    return first, logits, step, causal, cumulative, doc, entry, tail, passes


def fetch(refs, held, sems):
    parts = sems.shape[1]
    width = held.shape[2] // parts
    copies = [
        [
            pltpu.make_async_copy(
                ref.at[0, :, pl.ds(p * width, width)], held.at[i, :, pl.ds(p * width, width)], sems.at[i, p]
            )
            for i, ref in enumerate(refs)
        ]
        for p in range(parts)
    ]
    for group in copies:
        for copy in group:
            copy.start()
    return copies


def states_kernel(
    query_ref, key_ref, value_ref, dout_ref, gate_ref, bias_ref, offsets_ref, pay_ref, held, sems
):
    heads = bias_ref.shape[1]
    parts = sems.shape[1]
    copies = fetch((query_ref, key_ref, value_ref, dout_ref), held, sems)
    _, _, _, _, cumulative, _, entry, tail, passes = decays(gate_ref, bias_ref, offsets_ref)
    coarse, fine = log_parts(jnp.where(passes, jnp.maximum(cumulative[-1:, :], -120.0), -128.0))
    powers = {}
    for h in range(heads):
        if h % (heads // parts) == 0:
            for copy in copies[h // (heads // parts)]:
                copy.wait()
        cols = matrix(h)
        one = slice(h, h + 1)
        slot, m = divmod(h, 2)
        for place, left, right, weight in (
            (m, 1, 2, tail[:, one]),
            (2 + m, 0, 3, entry[:, one] * SCALE),
        ):
            upper, lower = split2(held[left, :, cols].astype(F32) * weight)
            right = held[right, :, cols]
            steps, powers[place] = encode(tn(upper, right) + tn(lower, right))
            pay_ref[slot, matrix(place), :] = whole16(steps)
        if m == 1:
            pay_ref[slot, tail_of(pay_ref), :] = rows16(
                *(powers[i] for i in range(4)),
                *(x[:, i : i + 1] for i in (h - 1, h) for x in (coarse, fine)),
            )


def totals_kernel(pay_ref, *send_refs):
    count = pay_ref.shape[0]
    tails = [wide(pay_ref[c, tail_of(pay_ref), :]) for c in range(count)]
    mine, segments = lax.axis_index("seg"), lax.axis_size("seg")
    ends, logs = [], []
    for m in range(2):
        log = [log_whole(t[4 + 2 * m : 5 + 2 * m], t[5 + 2 * m : 6 + 2 * m]) for t in tails]
        for place, order in ((m, range(count)), (2 + m, range(count - 1, -1, -1))):
            carry = jnp.zeros((HEAD_DIM, HEAD_DIM), F32)
            for c in order:
                carry = jnp.exp(log[c]) * carry + decode(
                    pay_ref[c, matrix(place), :], tails[c][place : place + 1]
                )
            ends.append(encode(carry))
        logs.extend(log_parts(sum(log)))
    for distance, send_ref in enumerate(send_refs, 1):
        later = mine + distance < segments
        for m in range(2):
            send_ref[matrix(m), :] = whole16(jnp.where(later, ends[2 * m][0], ends[2 * m + 1][0]))
        send_ref[tail_of(send_ref), :] = rows16(
            *(jnp.where(later, ends[2 * m][1], ends[2 * m + 1][1]) for m in range(2)), *logs
        )


def scan_kernel(pay_ref, *refs):
    *got_refs, out_ref = refs
    count = pay_ref.shape[0]
    mine = lax.axis_index("seg")
    tails = [wide(pay_ref[c, tail_of(pay_ref), :]) for c in range(count)]
    got_tails = [wide(ref[tail_of(ref), :]) for ref in got_refs]
    powers = [[None] * 4 for _ in range(count)]
    for m in range(2):
        log = [log_whole(t[4 + 2 * m : 5 + 2 * m], t[5 + 2 * m : 6 + 2 * m]) for t in tails]
        sent = [
            (jnp.exp(log_whole(t[2 + 2 * m : 3 + 2 * m], t[3 + 2 * m : 4 + 2 * m])), decode(ref[matrix(m), :], t[m : m + 1]))
            for ref, t in zip(got_refs, got_tails)
        ]
        state = jnp.zeros((HEAD_DIM, HEAD_DIM), F32)
        for d in range(len(sent), 0, -1):
            state = jnp.where(mine >= d, sent[d - 1][0] * state + sent[d - 1][1], state)
        grad = jnp.zeros((HEAD_DIM, HEAD_DIM), F32)
        for d in range(1, len(sent) + 1):
            grad = jnp.where(mine < d, sent[d - 1][0] * grad + sent[d - 1][1], grad)
        for place, carry, order in ((m, state, range(count)), (2 + m, grad, range(count - 1, -1, -1))):
            for i, c in enumerate(order):
                steps, powers[c][place] = encode(carry)
                out_ref[c, matrix(place), :] = whole16(steps)
                if i < count - 1:
                    carry = jnp.exp(log[c]) * carry + decode(
                        pay_ref[c, matrix(place), :], tails[c][place : place + 1]
                    )
    for c in range(count):
        out_ref[c, tail_of(out_ref), :] = rows16(*powers[c])


def local_kernel(
    query_ref, key_ref, value_ref, dout_ref, gate_ref, bias_ref, offsets_ref,
    dq_ref, dk_ref, dv_ref, sums_ref, held, sems,
):
    heads, length = gate_ref.shape[1:]
    parts = sems.shape[1]
    copies = fetch((query_ref, key_ref, value_ref, dout_ref), held, sems)
    first, _, step, causal, cumulative, doc, _, _, _ = decays(gate_ref, bias_ref, offsets_ref)
    cumulative_row = nt(step, causal.astype(F32), HIGHEST)
    linked = causal & (doc == doc_of(first + iota((1, length), 1), offsets_ref))
    lane = iota((length, heads), 1)
    sublane = iota((heads, length), 0)
    ends = jnp.zeros((length, heads), F32)
    ends_row = jnp.zeros((heads, length), F32)
    for h in range(heads):
        if h % (heads // parts) == 0:
            for copy in copies[h // (heads // parts)]:
                copy.wait()
        cols = matrix(h)
        q, k, v, d = (held[i, :, cols] for i in range(4))
        weights = jnp.where(
            linked,
            jnp.exp(jnp.where(linked, cumulative[:, h : h + 1] - cumulative_row[h : h + 1, :], 0.0)),
            0.0,
        ) * SCALE
        probs = nt(q, k) * weights
        dprobs = nt(d, v)
        pairs = probs * dprobs
        probs = probs.astype(BF16)
        dscores = (dprobs * weights).astype(BF16)
        dq_ref[:, cols] = nn(dscores, k)
        dk_ref[:, cols] = tn(dscores, q)
        dv_ref[:, cols] = tn(probs, d)
        ends = jnp.where(lane == h, jnp.sum(pairs, axis=1, keepdims=True), ends)
        ends_row = jnp.where(sublane == h, jnp.sum(pairs, axis=0, keepdims=True), ends_row)
    causal = causal.astype(F32)
    sums_ref[...] = tn(ends, causal, HIGHEST) - nn(ends_row, causal, HIGHEST)


def gates_kernel(
    query_ref, key_ref, value_ref, dout_ref, gate_ref, bias_ref, offsets_ref, sums_ref, state_ref,
    dgate_ref, dbias_ref, held, sems,
):
    heads, length = gate_ref.shape[1:]
    parts = sems.shape[1]
    copies = fetch((query_ref, key_ref, value_ref, dout_ref), held, sems)
    _, logits, _, causal, cumulative, _, entry, tail, passes = decays(gate_ref, bias_ref, offsets_ref)
    lane = iota((length, heads), 1)
    same = iota((heads, heads), 0) == iota((heads, heads), 1)
    ends = jnp.zeros((length, heads), F32)
    starts = jnp.zeros((length, heads), F32)
    whole = jnp.zeros((1, heads), F32)
    for h in range(heads):
        if h % (heads // parts) == 0:
            for copy in copies[h // (heads // parts)]:
                copy.wait()
        cols = matrix(h)
        one = slice(h, h + 1)
        slot, m = divmod(h, 2)
        powers = wide(state_ref[slot, tail_of(state_ref), :])
        state32, grad32 = (
            decode(state_ref[slot, matrix(place), :], powers[place : place + 1]) for place in (m, 2 + m)
        )
        state, state_low = split2(state32)
        grad, grad_low = split2(grad32)
        q, k, v, d = (held[i, :, cols] for i in range(4))
        dq = (entry[:, one] * SCALE) * (nt(d, state) + nt(d, state_low))
        dk = tail[:, one] * (nt(v, grad) + nt(v, grad_low))
        at_end = jnp.sum(q.astype(F32) * dq, axis=1, keepdims=True)
        at_start = jnp.sum(k.astype(F32) * dk, axis=1, keepdims=True)
        ends = jnp.where(lane == h, at_end, ends)
        starts = jnp.where(lane == h, at_start, starts)
        whole = jnp.where(lane[0:1] == h, jnp.sum(state32 * grad32, keepdims=True), whole)
    through = jnp.where(passes, jnp.exp(cumulative[length - 1 :, :]), 0.0) * whole
    earlier = (iota((length, length), 0) < iota((length, length), 1)).astype(F32)
    dstep = (
        sums_ref[...]
        + tn(ends, causal.astype(F32), HIGHEST)
        + tn(starts, earlier, HIGHEST)
        + jnp.sum(jnp.where(same, through, 0.0), axis=1, keepdims=True)
    )
    dlogit = -dstep / (1.0 + jnp.exp(-logits))
    dgate_ref[0] = dlogit.astype(BF16)
    dbias_ref[...] = jnp.sum(
        jnp.where(same, jnp.sum(dlogit, axis=1, keepdims=True), 0.0), axis=0, keepdims=True
    )


def output_kernel(
    key_ref, value_ref, dout_ref, gate_ref, bias_ref, offsets_ref, state_ref, dq_near_ref, dk_near_ref,
    dv_near_ref, dq_ref, dk_ref, dv_ref,
):
    heads = bias_ref.shape[1]
    _, _, _, _, _, _, entry, tail, _ = decays(gate_ref, bias_ref, offsets_ref)
    for h in range(heads):
        cols = matrix(h)
        one = slice(h, h + 1)
        slot, m = divmod(h, 2)
        powers = wide(state_ref[slot, tail_of(state_ref), :])
        state, grad = (
            decode(state_ref[slot, matrix(place), :], powers[place : place + 1]).astype(BF16)
            for place in (m, 2 + m)
        )
        for near_ref, out_ref, far, decay in (
            (dq_near_ref, dq_ref, nt(dout_ref[0, :, cols], state), entry[:, one] * SCALE),
            (dk_near_ref, dk_ref, nt(value_ref[0, :, cols], grad), tail[:, one]),
            (dv_near_ref, dv_ref, nn(key_ref[0, :, cols], grad), tail[:, one]),
        ):
            out_ref[0, :, cols] = (near_ref[:, cols] + decay * far).astype(BF16)


def call(kernel, out_shape, in_specs, **more):
    several = isinstance(out_shape, tuple)
    return pl.pallas_call(
        kernel,
        out_shape=out_shape,
        in_specs=in_specs,
        out_specs=(VMEM,) * len(out_shape) if several else VMEM,
        compiler_params=PARAMS,
        **more,
    )


def shards(query, key, value, dout, gate_in, gate_bias, offsets):
    heads = gate_bias.shape[0]
    count, segments = lax.axis_size("grp"), lax.axis_size("seg")
    gates = jnp.swapaxes(gate_in, 1, 2)
    rest = (gates, gate_bias.reshape(1, heads), offsets)
    inputs = tuple(pltpu.with_memory_space_constraint(x, pltpu.HBM) for x in (query, key, value, dout)) + rest
    fetched = [HBM] * 4 + [VMEM] * 2 + [SMEM]
    scratch = [pltpu.VMEM((4,) + query.shape[1:], BF16), pltpu.SemaphoreType.DMA((4, 4))]
    packed = jax.ShapeDtypeStruct((count, 4 * HEAD_DIM + TAIL, LANES), I16)
    pay = call(
        states_kernel,
        packed,
        fetched,
        scratch_shapes=scratch,
    )(*inputs)
    pay = lax.all_to_all(pay, "grp", split_axis=0, concat_axis=0, tiled=True)
    total = jax.ShapeDtypeStruct((2 * HEAD_DIM + TAIL, LANES), I16)
    sends = call(totals_kernel, (total,) * (segments - 1), [VMEM])(pay)
    got = [
        lax.ppermute(send, "seg", [(i, (i + d) % segments) for i in range(segments)])
        for d, send in enumerate(sends, 1)
    ]
    carried = call(scan_kernel, packed, [VMEM] * segments)(pay, *got)
    carried = lax.all_to_all(carried, "grp", split_axis=0, concat_axis=0, tiled=True)
    wide_like = jax.ShapeDtypeStruct(query.shape[1:], F32)
    sums_like = jax.ShapeDtypeStruct(gates.shape[1:], F32)
    *near, sums = call(local_kernel, (wide_like,) * 3 + (sums_like,), fetched, scratch_shapes=scratch)(*inputs)
    dgate, dbias = call(
        gates_kernel,
        (jax.ShapeDtypeStruct(gates.shape, BF16), jax.ShapeDtypeStruct((1, heads), F32)),
        fetched + [VMEM, VMEM],
        scratch_shapes=scratch,
    )(*inputs, sums, carried)
    everywhere = lax.all_to_all(
        jnp.broadcast_to(dbias[None], (lax.axis_size(ALL), 1, heads)), ALL, split_axis=0, concat_axis=0, tiled=True
    )
    like = jax.ShapeDtypeStruct(query.shape, BF16)
    dq, dk, dv = call(output_kernel, (like,) * 3, [VMEM] * 5 + [SMEM] + [VMEM] * 4)(
        key, value, dout, *rest, carried, *near
    )
    return dq, dk, dv, jnp.swapaxes(dgate, 1, 2), jnp.sum(everywhere, axis=(0, 1))


def solution(mesh):
    rows = P("dp", LINE, None)
    return jax.shard_map(
        shards,
        mesh=mesh,
        in_specs=(rows, rows, rows, rows, rows, P(), P("dp", None)),
        out_specs=(rows, rows, rows, rows, P()),
        check_vma=False,
    )
```

```python
import jax
import jax.numpy as jnp
from jax import lax
from jax.experimental import pallas as pl
from jax.experimental.pallas import tpu as pltpu
from jax.sharding import PartitionSpec as P

HEAD_DIM = 128
SCALE = HEAD_DIM ** (-0.5)
DOCS = 4
LINE = ("seg", "grp")
ALL = ("dp", "seg", "grp")
TAIL = 16
LANES = 128
F32 = jnp.float32
BF16 = jnp.bfloat16
I16 = jnp.int16
VMEM = pl.BlockSpec(memory_space=pltpu.VMEM)
SMEM = pl.BlockSpec(memory_space=pltpu.SMEM)
HBM = pl.BlockSpec(memory_space=pltpu.HBM)
HIGHEST = lax.Precision.HIGHEST
PARAMS = pltpu.CompilerParams(vmem_limit_bytes=20 * 1024 * 1024)


def dot(a, b, over, precision=None):
    return lax.dot_general(
        a, b, (((over[0],), (over[1],)), ((), ())), precision=precision, preferred_element_type=F32
    )


def nn(a, b, precision=None):
    return dot(a, b, (1, 0), precision)


def nt(a, b, precision=None):
    return dot(a, b, (1, 1), precision)


def tn(a, b, precision=None):
    return dot(a, b, (0, 0), precision)


def split2(x):
    hi = x.astype(BF16)
    return hi, (x - hi.astype(F32)).astype(BF16)


def matrix(m):
    return pl.ds(m * HEAD_DIM, HEAD_DIM)


def tail_of(ref):
    return pl.ds(ref.shape[-2] - TAIL, TAIL)


def iota(shape, dim):
    return lax.broadcasted_iota(jnp.int32, shape, dim)


def whole16(x):
    return x.astype(jnp.int32).astype(I16)


def wide(x):
    return x.astype(jnp.int32).astype(F32)


def encode(x):
    top = jnp.maximum(jnp.max(jnp.abs(x), axis=0, keepdims=True), 1e-30)
    power = jnp.ceil(jnp.log2(top) * 8.0)
    return jnp.clip(jnp.floor(x * jnp.exp2(15.0 - power / 8.0) + 0.5), -32767.0, 32767.0), power


def decode(steps, power):
    return wide(steps) * jnp.exp2(power / 8.0 - 15.0)


def encode2(x):
    power = jnp.ceil(jnp.log2(jnp.maximum(jnp.abs(x), 1e-30)))
    scaled = x * jnp.exp2(14.0 - power)
    high = jnp.floor(scaled + 0.5)
    return power, high, jnp.floor((scaled - high) * 16384.0 + 0.5)


def decode2(power, high, low):
    return (high + low / 16384.0) * jnp.exp2(power - 14.0)


def log_parts(log):
    coarse = jnp.floor(log * 256.0 + 0.5)
    return coarse, jnp.floor((log - coarse / 256.0) * 8388608.0 + 0.5)


def log_whole(coarse, fine):
    return coarse / 256.0 + fine / 8388608.0


def rows16(*rows):
    at = iota((TAIL, LANES), 0)
    total = jnp.zeros((TAIL, LANES), F32)
    for i, row in enumerate(rows):
        total = jnp.where(at == i, row, total)
    return whole16(total)


def doc_of(pos, offsets_ref):
    total = (pos >= offsets_ref[0, 0]).astype(jnp.int32)
    for i in range(1, DOCS):
        total = total + (pos >= offsets_ref[0, i]).astype(jnp.int32)
    return total


def place():
    return lax.axis_index("seg") * lax.axis_size("grp") + lax.axis_index("grp")


def decays(gates, bias, offsets_ref):
    heads, length = gates.shape
    first = place() * length
    same = iota((heads, heads), 0) == iota((heads, heads), 1)
    logits = gates.astype(F32) + jnp.sum(jnp.where(same, bias, 0.0), axis=1, keepdims=True)
    step = -(jnp.maximum(logits, 0.0) + jnp.log1p(jnp.exp(-jnp.abs(logits))))
    causal = iota((length, length), 0) >= iota((length, length), 1)
    cumulative = nt(causal.astype(F32), step, HIGHEST)
    doc = doc_of(first + iota((length, 1), 0), offsets_ref)
    doc_last = doc_of(first + length - 1, offsets_ref)
    before = jnp.where(first > 0, doc_of(first - 1, offsets_ref), -1)
    entry = jnp.exp(cumulative) * (doc == before).astype(F32)
    tail = jnp.exp(cumulative[length - 1 :, :] - cumulative) * (doc == doc_last).astype(F32)
    return first, logits, step, causal, cumulative, doc, entry, tail, doc_last == before


def fetch(refs, held, sems):
    parts = sems.shape[1]
    width = held.shape[2] // parts
    copies = [
        [
            pltpu.make_async_copy(
                ref.at[0, :, pl.ds(p * width, width)], held.at[i, :, pl.ds(p * width, width)], sems.at[i, p]
            )
            for i, ref in enumerate(refs)
        ]
        for p in range(parts)
    ]
    for group in copies:
        for copy in group:
            copy.start()
    return copies


def arrive(copies, head, heads):
    each = heads // len(copies)
    if head % each == 0:
        for copy in copies[head // each]:
            copy.wait()


def states_kernel(
    query_ref, key_ref, value_ref, dout_ref, gate_ref, bias_ref, offsets_ref,
    pay_ref, held, sems, gate_held, bias_held, offsets_held, small_sems,
):
    heads = bias_ref.shape[1]
    small = [
        pltpu.make_async_copy(gate_ref.at[0], gate_held, small_sems.at[0]),
        pltpu.make_async_copy(bias_ref, bias_held, small_sems.at[1]),
        pltpu.make_async_copy(offsets_ref, offsets_held, small_sems.at[2]),
    ]
    for copy in small:
        copy.start()
    copies = fetch((query_ref, key_ref, value_ref, dout_ref), held, sems)
    for copy in small:
        copy.wait()
    _, _, _, _, cumulative, _, entry, tail, passes = decays(gate_held[...], bias_held[...], offsets_held)
    coarse, fine = log_parts(jnp.where(passes, jnp.maximum(cumulative[-1:, :], -120.0), -128.0))
    powers = {}
    for h in range(heads):
        arrive(copies, h, heads)
        cols = matrix(h)
        one = slice(h, h + 1)
        slot, m = divmod(h, 2)
        for at, left, right, weight in ((m, 1, 2, tail[:, one]), (2 + m, 0, 3, entry[:, one] * SCALE)):
            upper, lower = split2(held[left, :, cols].astype(F32) * weight)
            right = held[right, :, cols]
            steps, powers[at] = encode(tn(upper, right) + tn(lower, right))
            pay_ref[slot, matrix(at), :] = whole16(steps)
        if m == 1:
            pay_ref[slot, tail_of(pay_ref), :] = rows16(
                *(powers[i] for i in range(4)),
                *(x[:, i : i + 1] for i in (h - 1, h) for x in (coarse, fine)),
            )


def chunk_logs(tails, m):
    return [log_whole(t[4 + 2 * m : 5 + 2 * m], t[5 + 2 * m : 6 + 2 * m]) for t in tails]


def totals_kernel(pay_ref, *send_refs):
    count = pay_ref.shape[0]
    tails = [wide(pay_ref[c, tail_of(pay_ref), :]) for c in range(count)]
    mine, segments = lax.axis_index("seg"), lax.axis_size("seg")
    at = iota((8, LANES), 0)
    logs = jnp.zeros((8, LANES), F32)
    for m in range(2):
        log = chunk_logs(tails, m)
        logs = jnp.where(at == m, sum(log), logs)
        ends = []
        for where, order in ((m, range(count)), (2 + m, range(count - 1, -1, -1))):
            carry = jnp.zeros((HEAD_DIM, HEAD_DIM), F32)
            for c in order:
                carry = jnp.exp(log[c]) * carry + decode(
                    pay_ref[c, matrix(where), :], tails[c][where : where + 1]
                )
            ends.append(carry)
        for distance, send_ref in enumerate(send_refs, 1):
            send_ref[matrix(m), :] = jnp.where(mine + distance < segments, *ends)
    for send_ref in send_refs:
        send_ref[pl.ds(2 * HEAD_DIM, 8), :] = logs


def scan_kernel(pay_ref, *refs):
    *got_refs, _, out_ref, held = refs
    count = pay_ref.shape[0]
    mine = lax.axis_index("seg")
    tails = [wide(pay_ref[c, tail_of(pay_ref), :]) for c in range(count)]
    at = iota((2 * count, LANES), 0)
    flows = jnp.zeros((2 * count, LANES), F32)
    powers = [[None] * 4 for _ in range(count)]
    for m in range(2):
        log = chunk_logs(tails, m)
        sent = [(jnp.exp(ref[pl.ds(2 * HEAD_DIM + m, 1), :]), ref[matrix(m), :]) for ref in got_refs]
        state = jnp.zeros((HEAD_DIM, HEAD_DIM), F32)
        for d in range(len(sent), 0, -1):
            state = jnp.where(mine >= d, sent[d - 1][0] * state + sent[d - 1][1], state)
        grad = jnp.zeros((HEAD_DIM, HEAD_DIM), F32)
        for d in range(1, len(sent) + 1):
            grad = jnp.where(mine < d, sent[d - 1][0] * grad + sent[d - 1][1], grad)
        for where, carry, order in ((m, state, range(count)), (2 + m, grad, range(count - 1, -1, -1))):
            for i, c in enumerate(order):
                steps, powers[c][where] = encode(carry)
                out_ref[c, matrix(where), :] = whole16(steps)
                passing = jnp.exp(log[c])
                if where == m:
                    held[c] = carry
                else:
                    flow = passing * jnp.sum(held[c] * carry, axis=0, keepdims=True)
                    flows = jnp.where(at == 2 * c + m, flow, flows)
                if i < count - 1:
                    carry = passing * carry + decode(pay_ref[c, matrix(where), :], tails[c][where : where + 1])
    parts = encode2(jnp.sum(flows, axis=1, keepdims=True))
    for c in range(count):
        out_ref[c, tail_of(out_ref), :] = rows16(
            *powers[c], *(part[2 * c + m : 2 * c + m + 1] for m in range(2) for part in parts)
        )


def local_kernel(
    query_ref, key_ref, value_ref, dout_ref, gate_ref, bias_ref, offsets_ref,
    dq_ref, dk_ref, dv_ref, rows_ref, cols_ref, held, sems,
):
    heads, length = gate_ref.shape[1:]
    copies = fetch((query_ref, key_ref, value_ref, dout_ref), held, sems)
    first, logits, step, causal, cumulative, doc, entry, tail, passes = decays(
        gate_ref[0], bias_ref[...], offsets_ref
    )
    cumulative_row = nt(step, causal.astype(F32), HIGHEST)
    linked = causal & (doc == doc_of(first + iota((1, length), 1), offsets_ref))
    lane = iota((length, heads), 1)
    sublane = iota((heads, length), 0)
    ends = jnp.zeros((length, heads), F32)
    ends_row = jnp.zeros((heads, length), F32)
    for h in range(heads):
        arrive(copies, h, heads)
        cols = matrix(h)
        q, k, v, d = (held[i, :, cols] for i in range(4))
        weights = jnp.where(
            linked,
            jnp.exp(jnp.where(linked, cumulative[:, h : h + 1] - cumulative_row[h : h + 1, :], 0.0)),
            0.0,
        ) * SCALE
        probs = nt(q, k) * weights
        dprobs = nt(d, v)
        pairs = probs * dprobs
        probs = probs.astype(BF16)
        dscores = (dprobs * weights).astype(BF16)
        dq_ref[:, cols] = nn(dscores, k)
        dk_ref[:, cols] = tn(dscores, q)
        dv_ref[:, cols] = tn(probs, d)
        ends = jnp.where(lane == h, jnp.sum(pairs, axis=1, keepdims=True), ends)
        ends_row = jnp.where(sublane == h, jnp.sum(pairs, axis=0, keepdims=True), ends_row)
    causal = causal.astype(F32)
    rows_ref[0] = tn(ends, causal, HIGHEST) - nn(ends_row, causal, HIGHEST)
    rows_ref[1] = -1.0 / (1.0 + jnp.exp(-logits))
    cols_ref[0] = entry * SCALE
    cols_ref[1] = tail


def received(state_ref, head):
    slot, m = divmod(head, 2)
    tail = wide(state_ref[slot, tail_of(state_ref), :])
    pair = tuple(decode(state_ref[slot, matrix(i), :], tail[i : i + 1]) for i in (m, 2 + m))
    return *pair, decode2(*(tail[i : i + 1, :1] for i in range(4 + 3 * m, 7 + 3 * m)))


def gates_kernel(
    query_ref, key_ref, value_ref, dout_ref, rows_ref, cols_ref, state_ref, dgate_ref, dbias_ref
):
    heads, length = dgate_ref.shape[1:]
    lane = iota((length, heads), 1)
    sublane = iota((heads, 1), 0)
    ends = jnp.zeros((length, heads), F32)
    starts = jnp.zeros((length, heads), F32)
    flows = jnp.zeros((heads, 1), F32)
    for h in range(heads):
        state32, grad32, flow = received(state_ref, h)
        state, state_low = split2(state32)
        grad, grad_low = split2(grad32)
        q, k, v, d = (ref[0, :, matrix(h)] for ref in (query_ref, key_ref, value_ref, dout_ref))
        at_end = jnp.sum(q.astype(F32) * (nt(d, state) + nt(d, state_low)), axis=1, keepdims=True)
        at_start = jnp.sum(k.astype(F32) * (nt(v, grad) + nt(v, grad_low)), axis=1, keepdims=True)
        ends = jnp.where(lane == h, at_end, ends)
        starts = jnp.where(lane == h, at_start, starts)
        flows = jnp.where(sublane == h, flow, flows)
    behind = iota((length, length), 0) - iota((length, length), 1)
    dstep = (
        rows_ref[0]
        + tn(ends * cols_ref[0], (behind >= 0).astype(F32), HIGHEST)
        + tn(starts * cols_ref[1], (behind < 0).astype(F32), HIGHEST)
        + flows
    )
    dlogit = dstep * rows_ref[1]
    dgate_ref[0] = dlogit.astype(BF16)
    same = iota((heads, heads), 0) == iota((heads, heads), 1)
    total = jnp.sum(jnp.where(same, jnp.sum(dlogit, axis=1, keepdims=True), 0.0), axis=0, keepdims=True)
    dbias_ref[...] = jnp.broadcast_to(total[None], dbias_ref.shape)


def output_kernel(
    key_ref, value_ref, dout_ref, cols_ref, state_ref, dq_near_ref, dk_near_ref, dv_near_ref,
    dq_ref, dk_ref, dv_ref,
):
    for h in range(cols_ref.shape[2]):
        cols = matrix(h)
        entry, tail = (cols_ref[i, :, h : h + 1] for i in range(2))
        state, grad = (x.astype(BF16) for x in received(state_ref, h)[:2])
        for near_ref, out_ref, far, decay in (
            (dq_near_ref, dq_ref, nt(dout_ref[0, :, cols], state), entry),
            (dk_near_ref, dk_ref, nt(value_ref[0, :, cols], grad), tail),
            (dv_near_ref, dv_ref, nn(key_ref[0, :, cols], grad), tail),
        ):
            out_ref[0, :, cols] = (near_ref[:, cols] + decay * far).astype(BF16)


def call(kernel, out_shape, in_specs, **more):
    several = isinstance(out_shape, tuple)
    return pl.pallas_call(
        kernel,
        out_shape=out_shape,
        in_specs=in_specs,
        out_specs=(VMEM,) * len(out_shape) if several else VMEM,
        compiler_params=PARAMS,
        **more,
    )


def shards(query, key, value, dout, gate_in, gate_bias, offsets):
    heads = gate_bias.shape[0]
    length, width = query.shape[1:]
    count, segments = lax.axis_size("grp"), lax.axis_size("seg")
    gates = jnp.swapaxes(gate_in, 1, 2)
    small = (gates, gate_bias.reshape(1, heads), offsets)
    pin = lambda xs: tuple(pltpu.with_memory_space_constraint(x, pltpu.HBM) for x in xs)
    big = pin((query, key, value, dout))
    scratch = [pltpu.VMEM((4, length, width), BF16), pltpu.SemaphoreType.DMA((4, 8))]
    packed = jax.ShapeDtypeStruct((count, 4 * HEAD_DIM + TAIL, LANES), I16)
    pay = call(
        states_kernel,
        packed,
        [HBM] * 7,
        scratch_shapes=scratch
        + [
            pltpu.VMEM((heads, length), BF16),
            pltpu.VMEM((1, heads), F32),
            pltpu.SMEM(offsets.shape, jnp.int32),
            pltpu.SemaphoreType.DMA((3,)),
        ],
    )(*big, *pin(small))
    pay = lax.all_to_all(pay, "grp", split_axis=0, concat_axis=0, tiled=True)
    total = jax.ShapeDtypeStruct((2 * HEAD_DIM + 8, LANES), F32)
    sends = call(totals_kernel, (total,) * (segments - 1), [VMEM])(pay)
    got = [
        lax.ppermute(send, "seg", [(i, (i + d) % segments) for i in range(segments)])
        for d, send in enumerate(sends, 1)
    ]
    near_like = jax.ShapeDtypeStruct((length, width), F32)
    *near, rows, cols = call(
        local_kernel,
        (near_like,) * 3
        + (jax.ShapeDtypeStruct((2, heads, length), F32), jax.ShapeDtypeStruct((2, length, heads), F32)),
        [HBM] * 4 + [VMEM] * 2 + [SMEM],
        scratch_shapes=scratch,
    )(*big, *small)
    carried = call(
        scan_kernel,
        packed,
        [VMEM] * segments + [pl.BlockSpec(memory_space=pl.ANY)],
        scratch_shapes=[pltpu.VMEM((count, HEAD_DIM, LANES), F32)],
    )(pay, *got, rows)
    carried = lax.all_to_all(carried, "grp", split_axis=0, concat_axis=0, tiled=True)
    dgate, dbias = call(
        gates_kernel,
        (
            jax.ShapeDtypeStruct(gates.shape, BF16),
            jax.ShapeDtypeStruct((lax.axis_size(ALL), 1, heads), F32),
        ),
        [VMEM] * 7,
    )(query, key, value, dout, rows, cols, carried)
    everywhere = lax.all_to_all(dbias, ALL, split_axis=0, concat_axis=0, tiled=True)
    like = jax.ShapeDtypeStruct(query.shape, BF16)
    dq, dk, dv = call(output_kernel, (like,) * 3, [VMEM] * 8)(key, value, dout, cols, carried, *near)
    return dq, dk, dv, jnp.swapaxes(dgate, 1, 2), jnp.sum(everywhere, axis=(0, 1))


def solution(mesh):
    rows = P("dp", LINE, None)
    return jax.shard_map(
        shards,
        mesh=mesh,
        in_specs=(rows, rows, rows, rows, rows, P(), P("dp", None)),
        out_specs=(rows, rows, rows, rows, P()),
        check_vma=False,
    )
```

```python
import jax
import jax.numpy as jnp
from jax import lax
from jax.experimental import pallas as pl
from jax.experimental.pallas import tpu as pltpu
from jax.sharding import PartitionSpec as P

HEAD_DIM = 128
SCALE = HEAD_DIM ** (-0.5)
DOCS = 4
LINE = ("seg", "grp")
ALL = ("dp", "seg", "grp")
TAIL = 16
LANES = 128
F32 = jnp.float32
BF16 = jnp.bfloat16
I16 = jnp.int16
VMEM = pl.BlockSpec(memory_space=pltpu.VMEM)
SMEM = pl.BlockSpec(memory_space=pltpu.SMEM)
HBM = pl.BlockSpec(memory_space=pltpu.HBM)
HIGHEST = lax.Precision.HIGHEST
PARAMS = pltpu.CompilerParams(vmem_limit_bytes=20 * 1024 * 1024)


def dot(a, b, over, precision=None):
    return lax.dot_general(
        a, b, (((over[0],), (over[1],)), ((), ())), precision=precision, preferred_element_type=F32
    )


def nn(a, b, precision=None):
    return dot(a, b, (1, 0), precision)


def nt(a, b, precision=None):
    return dot(a, b, (1, 1), precision)


def tn(a, b, precision=None):
    return dot(a, b, (0, 0), precision)


def split2(x):
    hi = x.astype(BF16)
    return hi, (x - hi.astype(F32)).astype(BF16)


def matrix(m):
    return pl.ds(m * HEAD_DIM, HEAD_DIM)


def tail_of(ref):
    return pl.ds(ref.shape[-2] - TAIL, TAIL)


def iota(shape, dim):
    return lax.broadcasted_iota(jnp.int32, shape, dim)


def whole16(x):
    return x.astype(jnp.int32).astype(I16)


def wide(x):
    return x.astype(jnp.int32).astype(F32)


def encode(x):
    top = jnp.maximum(jnp.max(jnp.abs(x), axis=0, keepdims=True), 1e-30)
    power = jnp.ceil(jnp.log2(top) * 8.0)
    return jnp.clip(jnp.floor(x * jnp.exp2(15.0 - power / 8.0) + 0.5), -32767.0, 32767.0), power


def decode(steps, power):
    return wide(steps) * jnp.exp2(power / 8.0 - 15.0)


def encode2(x):
    power = jnp.ceil(jnp.log2(jnp.maximum(jnp.abs(x), 1e-30)))
    scaled = x * jnp.exp2(14.0 - power)
    high = jnp.floor(scaled + 0.5)
    return power, high, jnp.floor((scaled - high) * 16384.0 + 0.5)


def decode2(power, high, low):
    return (high + low / 16384.0) * jnp.exp2(power - 14.0)


def log_parts(log):
    coarse = jnp.floor(log * 256.0 + 0.5)
    return coarse, jnp.floor((log - coarse / 256.0) * 8388608.0 + 0.5)


def log_whole(coarse, fine):
    return coarse / 256.0 + fine / 8388608.0


def rows16(*rows):
    at = iota((TAIL, LANES), 0)
    total = jnp.zeros((TAIL, LANES), F32)
    for i, row in enumerate(rows):
        total = jnp.where(at == i, row, total)
    return whole16(total)


def doc_of(pos, offsets_ref):
    total = (pos >= offsets_ref[0, 0]).astype(jnp.int32)
    for i in range(1, DOCS):
        total = total + (pos >= offsets_ref[0, i]).astype(jnp.int32)
    return total


def place():
    return lax.axis_index("seg") * lax.axis_size("grp") + lax.axis_index("grp")


def decays(gates, bias, offsets_ref):
    heads, length = gates.shape
    first = place() * length
    same = iota((heads, heads), 0) == iota((heads, heads), 1)
    logits = gates.astype(F32) + jnp.sum(jnp.where(same, bias, 0.0), axis=1, keepdims=True)
    step = -(jnp.maximum(logits, 0.0) + jnp.log1p(jnp.exp(-jnp.abs(logits))))
    causal = iota((length, length), 0) >= iota((length, length), 1)
    cumulative = nt(causal.astype(F32), step, HIGHEST)
    doc = doc_of(first + iota((length, 1), 0), offsets_ref)
    doc_last = doc_of(first + length - 1, offsets_ref)
    before = jnp.where(first > 0, doc_of(first - 1, offsets_ref), -1)
    entry = jnp.exp(cumulative) * (doc == before).astype(F32)
    tail = jnp.exp(cumulative[length - 1 :, :] - cumulative) * (doc == doc_last).astype(F32)
    return first, logits, step, causal, cumulative, doc, entry, tail, doc_last == before


def fetch(refs, held, sems):
    parts = sems.shape[1]
    width = held.shape[2] // parts
    copies = [
        [
            pltpu.make_async_copy(
                ref.at[0, :, pl.ds(p * width, width)], held.at[i, :, pl.ds(p * width, width)], sems.at[i, p]
            )
            for i, ref in enumerate(refs)
        ]
        for p in range(parts)
    ]
    for group in copies:
        for copy in group:
            copy.start()
    return copies


def arrive(copies, head, heads):
    each = heads // len(copies)
    if head % each == 0:
        for copy in copies[head // each]:
            copy.wait()


def states_kernel(
    query_ref, key_ref, value_ref, dout_ref, gate_ref, bias_ref, offsets_ref,
    pay_ref, held, sems, gate_held, bias_held, offsets_held, small_sems,
):
    heads = bias_ref.shape[1]
    small = [
        pltpu.make_async_copy(gate_ref.at[0], gate_held, small_sems.at[0]),
        pltpu.make_async_copy(bias_ref, bias_held, small_sems.at[1]),
        pltpu.make_async_copy(offsets_ref, offsets_held, small_sems.at[2]),
    ]
    for copy in small:
        copy.start()
    copies = fetch((query_ref, key_ref, value_ref, dout_ref), held, sems)
    for copy in small:
        copy.wait()
    _, _, _, _, cumulative, _, entry, tail, passes = decays(gate_held[...], bias_held[...], offsets_held)
    coarse, fine = log_parts(jnp.where(passes, jnp.maximum(cumulative[-1:, :], -120.0), -128.0))
    powers = {}
    for h in range(heads):
        arrive(copies, h, heads)
        cols = matrix(h)
        one = slice(h, h + 1)
        slot, m = divmod(h, 2)
        for at, left, right, weight in ((m, 1, 2, tail[:, one]), (2 + m, 0, 3, entry[:, one] * SCALE)):
            upper, lower = split2(held[left, :, cols].astype(F32) * weight)
            right = held[right, :, cols]
            steps, powers[at] = encode(tn(upper, right) + tn(lower, right))
            pay_ref[slot, matrix(at), :] = whole16(steps)
        if m == 1:
            pay_ref[slot, tail_of(pay_ref), :] = rows16(
                *(powers[i] for i in range(4)),
                *(x[:, i : i + 1] for i in (h - 1, h) for x in (coarse, fine)),
            )


def chunk_logs(tails, m):
    return [log_whole(t[4 + 2 * m : 5 + 2 * m], t[5 + 2 * m : 6 + 2 * m]) for t in tails]


def totals_kernel(pay_ref, _, *send_refs):
    count = pay_ref.shape[0]
    tails = [wide(pay_ref[c, tail_of(pay_ref), :]) for c in range(count)]
    mine, segments = lax.axis_index("seg"), lax.axis_size("seg")
    at = iota((8, LANES), 0)
    logs = jnp.zeros((8, LANES), F32)
    for m in range(2):
        log = chunk_logs(tails, m)
        logs = jnp.where(at == m, sum(log), logs)
        ends = []
        for where, order in ((m, range(count)), (2 + m, range(count - 1, -1, -1))):
            carry = jnp.zeros((HEAD_DIM, HEAD_DIM), F32)
            for c in order:
                carry = jnp.exp(log[c]) * carry + decode(
                    pay_ref[c, matrix(where), :], tails[c][where : where + 1]
                )
            ends.append(carry)
        for distance, send_ref in enumerate(send_refs, 1):
            send_ref[matrix(m), :] = jnp.where(mine + distance < segments, *ends)
    for send_ref in send_refs:
        send_ref[pl.ds(2 * HEAD_DIM, 8), :] = logs


def scan_kernel(pay_ref, *refs):
    *got_refs, out_ref, held = refs
    count = pay_ref.shape[0]
    mine = lax.axis_index("seg")
    tails = [wide(pay_ref[c, tail_of(pay_ref), :]) for c in range(count)]
    at = iota((2 * count, LANES), 0)
    flows = jnp.zeros((2 * count, LANES), F32)
    powers = [[None] * 4 for _ in range(count)]
    for m in range(2):
        log = chunk_logs(tails, m)
        sent = [(jnp.exp(ref[pl.ds(2 * HEAD_DIM + m, 1), :]), ref[matrix(m), :]) for ref in got_refs]
        state = jnp.zeros((HEAD_DIM, HEAD_DIM), F32)
        for d in range(len(sent), 0, -1):
            state = jnp.where(mine >= d, sent[d - 1][0] * state + sent[d - 1][1], state)
        grad = jnp.zeros((HEAD_DIM, HEAD_DIM), F32)
        for d in range(1, len(sent) + 1):
            grad = jnp.where(mine < d, sent[d - 1][0] * grad + sent[d - 1][1], grad)
        for where, carry, order in ((m, state, range(count)), (2 + m, grad, range(count - 1, -1, -1))):
            for i, c in enumerate(order):
                steps, powers[c][where] = encode(carry)
                out_ref[c, matrix(where), :] = whole16(steps)
                passing = jnp.exp(log[c])
                if where == m:
                    held[c] = carry
                else:
                    flow = passing * jnp.sum(held[c] * carry, axis=0, keepdims=True)
                    flows = jnp.where(at == 2 * c + m, flow, flows)
                if i < count - 1:
                    carry = passing * carry + decode(pay_ref[c, matrix(where), :], tails[c][where : where + 1])
    parts = encode2(jnp.sum(flows, axis=1, keepdims=True))
    for c in range(count):
        out_ref[c, tail_of(out_ref), :] = rows16(
            *powers[c], *(part[2 * c + m : 2 * c + m + 1] for m in range(2) for part in parts)
        )


def local_kernel(
    query_ref, key_ref, value_ref, dout_ref, gate_ref, bias_ref, offsets_ref,
    dq_ref, dk_ref, dv_ref, rows_ref, cols_ref, held, sems,
):
    heads, length = gate_ref.shape[1:]
    copies = fetch((query_ref, key_ref, value_ref, dout_ref), held, sems)
    first, logits, step, causal, cumulative, doc, entry, tail, passes = decays(
        gate_ref[0], bias_ref[...], offsets_ref
    )
    cumulative_row = nt(step, causal.astype(F32), HIGHEST)
    linked = causal & (doc == doc_of(first + iota((1, length), 1), offsets_ref))
    lane = iota((length, heads), 1)
    sublane = iota((heads, length), 0)
    ends = jnp.zeros((length, heads), F32)
    ends_row = jnp.zeros((heads, length), F32)
    for h in range(heads):
        arrive(copies, h, heads)
        cols = matrix(h)
        q, k, v, d = (held[i, :, cols] for i in range(4))
        weights = jnp.where(
            linked,
            jnp.exp(jnp.where(linked, cumulative[:, h : h + 1] - cumulative_row[h : h + 1, :], 0.0)),
            0.0,
        ) * SCALE
        probs = nt(q, k) * weights
        dprobs = nt(d, v)
        pairs = probs * dprobs
        probs = probs.astype(BF16)
        dscores = (dprobs * weights).astype(BF16)
        dq_ref[:, cols] = nn(dscores, k)
        dk_ref[:, cols] = tn(dscores, q)
        dv_ref[:, cols] = tn(probs, d)
        ends = jnp.where(lane == h, jnp.sum(pairs, axis=1, keepdims=True), ends)
        ends_row = jnp.where(sublane == h, jnp.sum(pairs, axis=0, keepdims=True), ends_row)
    causal = causal.astype(F32)
    rows_ref[0] = tn(ends, causal, HIGHEST) - nn(ends_row, causal, HIGHEST)
    rows_ref[1] = -1.0 / (1.0 + jnp.exp(-logits))
    cols_ref[0] = entry * SCALE
    cols_ref[1] = tail


def received(state_ref, head):
    slot, m = divmod(head, 2)
    tail = wide(state_ref[slot, tail_of(state_ref), :])
    pair = tuple(decode(state_ref[slot, matrix(i), :], tail[i : i + 1]) for i in (m, 2 + m))
    return *pair, decode2(*(tail[i : i + 1, :1] for i in range(4 + 3 * m, 7 + 3 * m)))


def gates_kernel(
    query_ref, key_ref, value_ref, dout_ref, rows_ref, cols_ref, state_ref, dgate_ref, dbias_ref
):
    heads, length = dgate_ref.shape[1:]
    lane = iota((length, heads), 1)
    sublane = iota((heads, 1), 0)
    ends = jnp.zeros((length, heads), F32)
    starts = jnp.zeros((length, heads), F32)
    flows = jnp.zeros((heads, 1), F32)
    for h in range(heads):
        state32, grad32, flow = received(state_ref, h)
        state, state_low = split2(state32)
        grad, grad_low = split2(grad32)
        q, k, v, d = (ref[0, :, matrix(h)] for ref in (query_ref, key_ref, value_ref, dout_ref))
        at_end = jnp.sum(q.astype(F32) * (nt(d, state) + nt(d, state_low)), axis=1, keepdims=True)
        at_start = jnp.sum(k.astype(F32) * (nt(v, grad) + nt(v, grad_low)), axis=1, keepdims=True)
        ends = jnp.where(lane == h, at_end, ends)
        starts = jnp.where(lane == h, at_start, starts)
        flows = jnp.where(sublane == h, flow, flows)
    behind = iota((length, length), 0) - iota((length, length), 1)
    dstep = (
        rows_ref[0]
        + tn(ends * cols_ref[0], (behind >= 0).astype(F32), HIGHEST)
        + tn(starts * cols_ref[1], (behind < 0).astype(F32), HIGHEST)
        + flows
    )
    dlogit = dstep * rows_ref[1]
    dgate_ref[0] = dlogit.astype(BF16)
    same = iota((heads, heads), 0) == iota((heads, heads), 1)
    total = jnp.sum(jnp.where(same, jnp.sum(dlogit, axis=1, keepdims=True), 0.0), axis=0, keepdims=True)
    dbias_ref[...] = jnp.broadcast_to(total[None], dbias_ref.shape)


def output_kernel(
    key_ref, value_ref, dout_ref, cols_ref, state_ref, dq_near_ref, dk_near_ref, dv_near_ref,
    dq_ref, dk_ref, dv_ref,
):
    for h in range(cols_ref.shape[2]):
        cols = matrix(h)
        entry, tail = (cols_ref[i, :, h : h + 1] for i in range(2))
        state, grad = (x.astype(BF16) for x in received(state_ref, h)[:2])
        for near_ref, out_ref, far, decay in (
            (dq_near_ref, dq_ref, nt(dout_ref[0, :, cols], state), entry),
            (dk_near_ref, dk_ref, nt(value_ref[0, :, cols], grad), tail),
            (dv_near_ref, dv_ref, nn(key_ref[0, :, cols], grad), tail),
        ):
            out_ref[0, :, cols] = (near_ref[:, cols] + decay * far).astype(BF16)


def call(kernel, out_shape, in_specs, **more):
    several = isinstance(out_shape, tuple)
    return pl.pallas_call(
        kernel,
        out_shape=out_shape,
        in_specs=in_specs,
        out_specs=(VMEM,) * len(out_shape) if several else VMEM,
        compiler_params=PARAMS,
        **more,
    )


def shards(query, key, value, dout, gate_in, gate_bias, offsets):
    heads = gate_bias.shape[0]
    length, width = query.shape[1:]
    count, segments = lax.axis_size("grp"), lax.axis_size("seg")
    gates = jnp.swapaxes(gate_in, 1, 2)
    small = (gates, gate_bias.reshape(1, heads), offsets)
    pin = lambda xs: tuple(pltpu.with_memory_space_constraint(x, pltpu.HBM) for x in xs)
    big = pin((query, key, value, dout))
    scratch = [pltpu.VMEM((4, length, width), BF16), pltpu.SemaphoreType.DMA((4, 8))]
    packed = jax.ShapeDtypeStruct((count, 4 * HEAD_DIM + TAIL, LANES), I16)
    pay = call(
        states_kernel,
        packed,
        [HBM] * 7,
        scratch_shapes=scratch
        + [
            pltpu.VMEM((heads, length), BF16),
            pltpu.VMEM((1, heads), F32),
            pltpu.SMEM(offsets.shape, jnp.int32),
            pltpu.SemaphoreType.DMA((3,)),
        ],
    )(*big, *pin(small))
    pay = lax.all_to_all(pay, "grp", split_axis=0, concat_axis=0, tiled=True)
    near_like = jax.ShapeDtypeStruct((length, width), F32)
    *near, rows, cols = call(
        local_kernel,
        (near_like,) * 3
        + (jax.ShapeDtypeStruct((2, heads, length), F32), jax.ShapeDtypeStruct((2, length, heads), F32)),
        [HBM] * 4 + [VMEM] * 2 + [SMEM],
        scratch_shapes=scratch,
    )(*big, *small)
    total = jax.ShapeDtypeStruct((2 * HEAD_DIM + 8, LANES), F32)
    sends = call(totals_kernel, (total,) * (segments - 1), [VMEM, pl.BlockSpec(memory_space=pl.ANY)])(pay, rows)
    got = [
        lax.ppermute(send, "seg", [(i, (i + d) % segments) for i in range(segments)])
        for d, send in enumerate(sends, 1)
    ]
    carried = call(
        scan_kernel,
        packed,
        [VMEM] * segments,
        scratch_shapes=[pltpu.VMEM((count, HEAD_DIM, LANES), F32)],
    )(pay, *got)
    carried = lax.all_to_all(carried, "grp", split_axis=0, concat_axis=0, tiled=True)
    dgate, dbias = call(
        gates_kernel,
        (
            jax.ShapeDtypeStruct(gates.shape, BF16),
            jax.ShapeDtypeStruct((lax.axis_size(ALL), 1, heads), F32),
        ),
        [VMEM] * 7,
    )(query, key, value, dout, rows, cols, carried)
    everywhere = lax.all_to_all(dbias, ALL, split_axis=0, concat_axis=0, tiled=True)
    like = jax.ShapeDtypeStruct(query.shape, BF16)
    dq, dk, dv = call(output_kernel, (like,) * 3, [VMEM] * 8)(key, value, dout, cols, carried, *near)
    return dq, dk, dv, jnp.swapaxes(dgate, 1, 2), jnp.sum(everywhere, axis=(0, 1))


def solution(mesh):
    rows = P("dp", LINE, None)
    return jax.shard_map(
        shards,
        mesh=mesh,
        in_specs=(rows, rows, rows, rows, rows, P(), P("dp", None)),
        out_specs=(rows, rows, rows, rows, P()),
        check_vma=False,
    )
```

```python
import jax
import jax.numpy as jnp
from jax import lax
from jax.experimental import pallas as pl
from jax.experimental.pallas import tpu as pltpu
from jax.sharding import PartitionSpec as P

HEAD_DIM = 128
SCALE = HEAD_DIM ** (-0.5)
DOCS = 4
LINE = ("seg", "grp")
ALL = ("dp", "seg", "grp")
TAIL = 16
LANES = 128
F32 = jnp.float32
BF16 = jnp.bfloat16
I16 = jnp.int16
VMEM = pl.BlockSpec(memory_space=pltpu.VMEM)
SMEM = pl.BlockSpec(memory_space=pltpu.SMEM)
HBM = pl.BlockSpec(memory_space=pltpu.HBM)
HIGHEST = lax.Precision.HIGHEST
PARAMS = pltpu.CompilerParams(vmem_limit_bytes=20 * 1024 * 1024)


def dot(a, b, over, precision=None):
    return lax.dot_general(
        a, b, (((over[0],), (over[1],)), ((), ())), precision=precision, preferred_element_type=F32
    )


def nn(a, b, precision=None):
    return dot(a, b, (1, 0), precision)


def nt(a, b, precision=None):
    return dot(a, b, (1, 1), precision)


def tn(a, b, precision=None):
    return dot(a, b, (0, 0), precision)


def split2(x):
    hi = x.astype(BF16)
    return hi, (x - hi.astype(F32)).astype(BF16)


def tn2(a, b):
    both = tn(a, jnp.concatenate(split2(b), axis=1))
    return both[:, : b.shape[1]] + both[:, b.shape[1] :]


def nt2(a, b):
    both = nt(a, jnp.concatenate(split2(b), axis=0))
    return both[:, : b.shape[0]] + both[:, b.shape[0] :]


def matrix(m):
    return pl.ds(m * HEAD_DIM, HEAD_DIM)


def tail_of(ref):
    return pl.ds(ref.shape[-2] - TAIL, TAIL)


def iota(shape, dim):
    return lax.broadcasted_iota(jnp.int32, shape, dim)


def whole16(x):
    return x.astype(jnp.int32).astype(I16)


def wide(x):
    return x.astype(jnp.int32).astype(F32)


def encode(x):
    top = jnp.maximum(jnp.max(jnp.abs(x), axis=0, keepdims=True), 1e-30)
    power = jnp.ceil(jnp.log2(top) * 8.0)
    return jnp.clip(jnp.floor(x * jnp.exp2(15.0 - power / 8.0) + 0.5), -32767.0, 32767.0), power


def decode(steps, power):
    return wide(steps) * jnp.exp2(power / 8.0 - 15.0)


def encode2(x):
    power = jnp.ceil(jnp.log2(jnp.maximum(jnp.abs(x), 1e-30)))
    scaled = x * jnp.exp2(14.0 - power)
    high = jnp.floor(scaled + 0.5)
    return power, high, jnp.floor((scaled - high) * 16384.0 + 0.5)


def decode2(power, high, low):
    return (high + low / 16384.0) * jnp.exp2(power - 14.0)


def log_parts(log):
    coarse = jnp.floor(log * 256.0 + 0.5)
    return coarse, jnp.floor((log - coarse / 256.0) * 8388608.0 + 0.5)


def log_whole(coarse, fine):
    return coarse / 256.0 + fine / 8388608.0


def rows16(*rows):
    at = iota((TAIL, LANES), 0)
    total = jnp.zeros((TAIL, LANES), F32)
    for i, row in enumerate(rows):
        total = jnp.where(at == i, row, total)
    return whole16(total)


def doc_of(pos, offsets_ref):
    total = (pos >= offsets_ref[0, 0]).astype(jnp.int32)
    for i in range(1, DOCS):
        total = total + (pos >= offsets_ref[0, i]).astype(jnp.int32)
    return total


def place():
    return lax.axis_index("seg") * lax.axis_size("grp") + lax.axis_index("grp")


def decays(gates, bias, offsets_ref):
    heads, length = gates.shape
    first = place() * length
    same = iota((heads, heads), 0) == iota((heads, heads), 1)
    logits = gates.astype(F32) + jnp.sum(jnp.where(same, bias, 0.0), axis=1, keepdims=True)
    step = -(jnp.maximum(logits, 0.0) + jnp.log1p(jnp.exp(-jnp.abs(logits))))
    causal = iota((length, length), 0) >= iota((length, length), 1)
    cumulative = nt(causal.astype(F32), step, HIGHEST)
    doc = doc_of(first + iota((length, 1), 0), offsets_ref)
    doc_last = doc_of(first + length - 1, offsets_ref)
    before = jnp.where(first > 0, doc_of(first - 1, offsets_ref), -1)
    entry = jnp.exp(cumulative) * (doc == before).astype(F32)
    tail = jnp.exp(cumulative[length - 1 :, :] - cumulative) * (doc == doc_last).astype(F32)
    return first, logits, step, causal, cumulative, doc, entry, tail, doc_last == before


def fetch(refs, held, sems):
    parts = sems.shape[1]
    width = held.shape[2] // parts
    copies = [
        [
            pltpu.make_async_copy(
                ref.at[0, :, pl.ds(p * width, width)], held.at[i, :, pl.ds(p * width, width)], sems.at[i, p]
            )
            for i, ref in enumerate(refs)
        ]
        for p in range(parts)
    ]
    for group in copies:
        for copy in group:
            copy.start()
    return copies


def arrive(copies, head, heads):
    each = heads // len(copies)
    if head % each == 0:
        for copy in copies[head // each]:
            copy.wait()


def states_kernel(
    query_ref, key_ref, value_ref, dout_ref, gate_ref, bias_ref, offsets_ref,
    pay_ref, held, sems, gate_held, bias_held, offsets_held, small_sems, pay, pay_sems,
):
    heads = bias_ref.shape[1]
    small = [
        pltpu.make_async_copy(gate_ref.at[0], gate_held, small_sems.at[0]),
        pltpu.make_async_copy(bias_ref, bias_held, small_sems.at[1]),
        pltpu.make_async_copy(offsets_ref, offsets_held, small_sems.at[2]),
    ]
    for copy in small:
        copy.start()
    copies = fetch((query_ref, key_ref, value_ref, dout_ref), held, sems)
    for copy in small:
        copy.wait()
    _, _, _, _, cumulative, _, entry, tail, passes = decays(gate_held[...], bias_held[...], offsets_held)
    coarse, fine = log_parts(jnp.where(passes, jnp.maximum(cumulative[-1:, :], -120.0), -128.0))
    powers, sent = {}, []
    for h in range(heads):
        arrive(copies, h, heads)
        cols = matrix(h)
        one = slice(h, h + 1)
        slot, m = divmod(h, 2)
        for at, left, right, weight in ((m, 1, 2, tail[:, one]), (2 + m, 0, 3, entry[:, one] * SCALE)):
            own = tn2(held[left, :, cols], held[right, :, cols].astype(F32) * weight)
            steps, powers[at] = encode(own)
            pay[slot, matrix(at), :] = whole16(steps)
        if m == 1:
            pay[slot, tail_of(pay), :] = rows16(
                *(powers[i] for i in range(4)),
                *(x[:, i : i + 1] for i in (h - 1, h) for x in (coarse, fine)),
            )
            sent.append(pltpu.make_async_copy(pay.at[slot], pay_ref.at[slot], pay_sems.at[slot]))
            sent[-1].start()
    for copy in sent:
        copy.wait()


def chunk_logs(tails, m):
    return [log_whole(t[4 + 2 * m : 5 + 2 * m], t[5 + 2 * m : 6 + 2 * m]) for t in tails]


def totals_kernel(pay_ref, _, *send_refs):
    count = pay_ref.shape[0]
    tails = [wide(pay_ref[c, tail_of(pay_ref), :]) for c in range(count)]
    mine, segments = lax.axis_index("seg"), lax.axis_size("seg")
    at = iota((8, LANES), 0)
    logs = jnp.zeros((8, LANES), F32)
    for m in range(2):
        log = chunk_logs(tails, m)
        logs = jnp.where(at == m, sum(log), logs)
        ends = []
        for where, order in ((m, range(count)), (2 + m, range(count - 1, -1, -1))):
            carry = jnp.zeros((HEAD_DIM, HEAD_DIM), F32)
            for c in order:
                carry = jnp.exp(log[c]) * carry + decode(
                    pay_ref[c, matrix(where), :], tails[c][where : where + 1]
                )
            ends.append(carry)
        for distance, send_ref in enumerate(send_refs, 1):
            send_ref[matrix(m), :] = jnp.where(mine + distance < segments, *ends)
    for send_ref in send_refs:
        send_ref[pl.ds(2 * HEAD_DIM, 8), :] = logs


def scan_kernel(pay_ref, *refs):
    *got_refs, out_ref, held = refs
    count = pay_ref.shape[0]
    mine = lax.axis_index("seg")
    tails = [wide(pay_ref[c, tail_of(pay_ref), :]) for c in range(count)]
    at = iota((2 * count, LANES), 0)
    flows = jnp.zeros((2 * count, LANES), F32)
    powers = [[None] * 4 for _ in range(count)]
    for m in range(2):
        log = chunk_logs(tails, m)
        sent = [(jnp.exp(ref[pl.ds(2 * HEAD_DIM + m, 1), :]), ref[matrix(m), :]) for ref in got_refs]
        state = jnp.zeros((HEAD_DIM, HEAD_DIM), F32)
        for d in range(len(sent), 0, -1):
            state = jnp.where(mine >= d, sent[d - 1][0] * state + sent[d - 1][1], state)
        grad = jnp.zeros((HEAD_DIM, HEAD_DIM), F32)
        for d in range(1, len(sent) + 1):
            grad = jnp.where(mine < d, sent[d - 1][0] * grad + sent[d - 1][1], grad)
        for where, carry, order in ((m, state, range(count)), (2 + m, grad, range(count - 1, -1, -1))):
            for i, c in enumerate(order):
                steps, powers[c][where] = encode(carry)
                out_ref[c, matrix(where), :] = whole16(steps)
                passing = jnp.exp(log[c])
                if where == m:
                    held[c] = carry
                else:
                    flow = passing * jnp.sum(held[c] * carry, axis=0, keepdims=True)
                    flows = jnp.where(at == 2 * c + m, flow, flows)
                if i < count - 1:
                    carry = passing * carry + decode(pay_ref[c, matrix(where), :], tails[c][where : where + 1])
    parts = encode2(jnp.sum(flows, axis=1, keepdims=True))
    for c in range(count):
        out_ref[c, tail_of(out_ref), :] = rows16(
            *powers[c], *(part[2 * c + m : 2 * c + m + 1] for m in range(2) for part in parts)
        )


def local_kernel(
    query_ref, key_ref, value_ref, dout_ref, gate_ref, bias_ref, offsets_ref,
    dq_ref, dk_ref, dv_ref, rows_ref, cols_ref, held, sems,
):
    heads, length = gate_ref.shape[1:]
    copies = fetch((query_ref, key_ref, value_ref, dout_ref), held, sems)
    first, logits, step, causal, cumulative, doc, entry, tail, passes = decays(
        gate_ref[0], bias_ref[...], offsets_ref
    )
    cumulative_row = nt(step, causal.astype(F32), HIGHEST)
    linked = causal & (doc == doc_of(first + iota((1, length), 1), offsets_ref))
    lane = iota((length, heads), 1)
    sublane = iota((heads, length), 0)
    ends = jnp.zeros((length, heads), F32)
    ends_row = jnp.zeros((heads, length), F32)
    for h in range(heads):
        arrive(copies, h, heads)
        cols = matrix(h)
        q, k, v, d = (held[i, :, cols] for i in range(4))
        weights = jnp.where(
            linked,
            jnp.exp(jnp.where(linked, cumulative[:, h : h + 1] - cumulative_row[h : h + 1, :], 0.0)),
            0.0,
        ) * SCALE
        probs = nt(q, k) * weights
        dprobs = nt(d, v)
        pairs = probs * dprobs
        probs = probs.astype(BF16)
        dscores = (dprobs * weights).astype(BF16)
        dq_ref[:, cols] = nn(dscores, k)
        dk_ref[:, cols] = tn(dscores, q)
        dv_ref[:, cols] = tn(probs, d)
        ends = jnp.where(lane == h, jnp.sum(pairs, axis=1, keepdims=True), ends)
        ends_row = jnp.where(sublane == h, jnp.sum(pairs, axis=0, keepdims=True), ends_row)
    causal = causal.astype(F32)
    rows_ref[0] = tn(ends, causal, HIGHEST) - nn(ends_row, causal, HIGHEST)
    rows_ref[1] = -1.0 / (1.0 + jnp.exp(-logits))
    cols_ref[0] = entry * SCALE
    cols_ref[1] = tail


def received(state_ref, head):
    slot, m = divmod(head, 2)
    tail = wide(state_ref[slot, tail_of(state_ref), :])
    pair = tuple(decode(state_ref[slot, matrix(i), :], tail[i : i + 1]) for i in (m, 2 + m))
    return *pair, decode2(*(tail[i : i + 1, :1] for i in range(4 + 3 * m, 7 + 3 * m)))


def gates_kernel(
    query_ref, key_ref, value_ref, dout_ref, rows_ref, cols_ref, state_ref, dgate_ref, dbias_ref
):
    heads, length = dgate_ref.shape[1:]
    lane = iota((length, heads), 1)
    sublane = iota((heads, 1), 0)
    ends = jnp.zeros((length, heads), F32)
    starts = jnp.zeros((length, heads), F32)
    flows = jnp.zeros((heads, 1), F32)
    for h in range(heads):
        state32, grad32, flow = received(state_ref, h)
        q, k, v, d = (ref[0, :, matrix(h)] for ref in (query_ref, key_ref, value_ref, dout_ref))
        at_end = jnp.sum(q.astype(F32) * nt2(d, state32), axis=1, keepdims=True)
        at_start = jnp.sum(k.astype(F32) * nt2(v, grad32), axis=1, keepdims=True)
        ends = jnp.where(lane == h, at_end, ends)
        starts = jnp.where(lane == h, at_start, starts)
        flows = jnp.where(sublane == h, flow, flows)
    behind = iota((length, length), 0) - iota((length, length), 1)
    dstep = (
        rows_ref[0]
        + tn(ends * cols_ref[0], (behind >= 0).astype(F32), HIGHEST)
        + tn(starts * cols_ref[1], (behind < 0).astype(F32), HIGHEST)
        + flows
    )
    dlogit = dstep * rows_ref[1]
    dgate_ref[0] = dlogit.astype(BF16)
    same = iota((heads, heads), 0) == iota((heads, heads), 1)
    total = jnp.sum(jnp.where(same, jnp.sum(dlogit, axis=1, keepdims=True), 0.0), axis=0, keepdims=True)
    dbias_ref[...] = jnp.broadcast_to(total[None], dbias_ref.shape)


def output_kernel(
    key_ref, value_ref, dout_ref, cols_ref, state_ref, dq_near_ref, dk_near_ref, dv_near_ref,
    dq_ref, dk_ref, dv_ref,
):
    for h in range(cols_ref.shape[2]):
        cols = matrix(h)
        entry, tail = (cols_ref[i, :, h : h + 1] for i in range(2))
        state, grad = (x.astype(BF16) for x in received(state_ref, h)[:2])
        for near_ref, out_ref, far, decay in (
            (dq_near_ref, dq_ref, nt(dout_ref[0, :, cols], state), entry),
            (dk_near_ref, dk_ref, nt(value_ref[0, :, cols], grad), tail),
            (dv_near_ref, dv_ref, nn(key_ref[0, :, cols], grad), tail),
        ):
            out_ref[0, :, cols] = (near_ref[:, cols] + decay * far).astype(BF16)


def call(kernel, out_shape, in_specs, **more):
    more.setdefault("out_specs", (VMEM,) * len(out_shape) if isinstance(out_shape, tuple) else VMEM)
    return pl.pallas_call(
        kernel, out_shape=out_shape, in_specs=in_specs, compiler_params=PARAMS, **more
    )


def shards(query, key, value, dout, gate_in, gate_bias, offsets):
    heads = gate_bias.shape[0]
    length, width = query.shape[1:]
    count, segments = lax.axis_size("grp"), lax.axis_size("seg")
    gates = jnp.swapaxes(gate_in, 1, 2)
    small = (gates, gate_bias.reshape(1, heads), offsets)
    pin = lambda xs: tuple(pltpu.with_memory_space_constraint(x, pltpu.HBM) for x in xs)
    big = pin((query, key, value, dout))
    scratch = [pltpu.VMEM((4, length, width), BF16), pltpu.SemaphoreType.DMA((4, 8))]
    packed = jax.ShapeDtypeStruct((count, 4 * HEAD_DIM + TAIL, LANES), I16)
    pay = call(
        states_kernel,
        packed,
        [HBM] * 7,
        scratch_shapes=scratch
        + [
            pltpu.VMEM((heads, length), BF16),
            pltpu.VMEM((1, heads), F32),
            pltpu.SMEM(offsets.shape, jnp.int32),
            pltpu.SemaphoreType.DMA((3,)),
            pltpu.VMEM(packed.shape, I16),
            pltpu.SemaphoreType.DMA((count,)),
        ],
        out_specs=HBM,
    )(*big, *pin(small))
    pay = lax.all_to_all(pay, "grp", split_axis=0, concat_axis=0, tiled=True)
    near_like = jax.ShapeDtypeStruct((length, width), F32)
    *near, rows, cols = call(
        local_kernel,
        (near_like,) * 3
        + (jax.ShapeDtypeStruct((2, heads, length), F32), jax.ShapeDtypeStruct((2, length, heads), F32)),
        [HBM] * 4 + [VMEM] * 2 + [SMEM],
        scratch_shapes=scratch,
    )(*big, *small)
    total = jax.ShapeDtypeStruct((2 * HEAD_DIM + 8, LANES), F32)
    sends = call(totals_kernel, (total,) * (segments - 1), [VMEM, pl.BlockSpec(memory_space=pl.ANY)])(pay, rows)
    got = [
        lax.ppermute(send, "seg", [(i, (i + d) % segments) for i in range(segments)])
        for d, send in enumerate(sends, 1)
    ]
    carried = call(
        scan_kernel,
        packed,
        [VMEM] * segments,
        scratch_shapes=[pltpu.VMEM((count, HEAD_DIM, LANES), F32)],
    )(pay, *got)
    carried = lax.all_to_all(carried, "grp", split_axis=0, concat_axis=0, tiled=True)
    dgate, dbias = call(
        gates_kernel,
        (
            jax.ShapeDtypeStruct(gates.shape, BF16),
            jax.ShapeDtypeStruct((lax.axis_size(ALL), 1, heads), F32),
        ),
        [VMEM] * 7,
    )(query, key, value, dout, rows, cols, carried)
    everywhere = lax.all_to_all(dbias, ALL, split_axis=0, concat_axis=0, tiled=True)
    like = jax.ShapeDtypeStruct(query.shape, BF16)
    dq, dk, dv = call(output_kernel, (like,) * 3, [VMEM] * 8)(key, value, dout, cols, carried, *near)
    return dq, dk, dv, jnp.swapaxes(dgate, 1, 2), jnp.sum(everywhere, axis=(0, 1))


def solution(mesh):
    rows = P("dp", LINE, None)
    return jax.shard_map(
        shards,
        mesh=mesh,
        in_specs=(rows, rows, rows, rows, rows, P(), P("dp", None)),
        out_specs=(rows, rows, rows, rows, P()),
        check_vma=False,
    )
```

```python
import jax
import jax.numpy as jnp
from jax import lax
from jax.experimental import pallas as pl
from jax.experimental.pallas import tpu as pltpu
from jax.sharding import PartitionSpec as P

HEAD_DIM = 128
SCALE = HEAD_DIM ** (-0.5)
DOCS = 4
LINE = ("seg", "grp")
ALL = ("dp", "seg", "grp")
TAIL = 16
LANES = 128
EXTRA = HEAD_DIM // 8
SLOT = 4 * HEAD_DIM + 4 * EXTRA + TAIL
F32 = jnp.float32
BF16 = jnp.bfloat16
I16 = jnp.int16
VMEM = pl.BlockSpec(memory_space=pltpu.VMEM)
SMEM = pl.BlockSpec(memory_space=pltpu.SMEM)
HBM = pl.BlockSpec(memory_space=pltpu.HBM)
HIGHEST = lax.Precision.HIGHEST
PARAMS = pltpu.CompilerParams(vmem_limit_bytes=20 * 1024 * 1024)


def dot(a, b, over, precision=None):
    return lax.dot_general(
        a, b, (((over[0],), (over[1],)), ((), ())), precision=precision, preferred_element_type=F32
    )


def nn(a, b, precision=None):
    return dot(a, b, (1, 0), precision)


def nt(a, b, precision=None):
    return dot(a, b, (1, 1), precision)


def tn(a, b, precision=None):
    return dot(a, b, (0, 0), precision)


def split2(x):
    hi = x.astype(BF16)
    return hi, (x - hi.astype(F32)).astype(BF16)


def tn2(a, b):
    both = tn(a, jnp.concatenate(split2(b), axis=1))
    return both[:, : b.shape[1]] + both[:, b.shape[1] :]


def nt2(a, b):
    both = nt(a, jnp.concatenate(split2(b), axis=0))
    return both[:, : b.shape[0]] + both[:, b.shape[0] :]


def matrix(m):
    return pl.ds(m * HEAD_DIM, HEAD_DIM)


def tail_of(ref):
    return pl.ds(ref.shape[-2] - TAIL, TAIL)


def extra(m):
    return pl.ds(4 * HEAD_DIM + m * EXTRA, EXTRA)


def iota(shape, dim):
    return lax.broadcasted_iota(jnp.int32, shape, dim)


def whole16(x):
    return x.astype(jnp.int32).astype(I16)


def wide(x):
    return x.astype(jnp.int32).astype(F32)


def encode(x, ref, at, *slot):
    top = jnp.maximum(jnp.max(jnp.abs(x), axis=0, keepdims=True), 1e-30)
    power = jnp.ceil(jnp.log2(top) * 8.0)
    steps = jnp.clip(jnp.floor(x * jnp.exp2(17.0 - power / 8.0) + 0.5), -131071.0, 131071.0)
    high = jnp.floor(steps * 0.25)
    low = steps - 4.0 * high
    packed = sum(low[k * EXTRA : (k + 1) * EXTRA] * 4.0**k for k in range(8))
    ref[*slot, matrix(at), :] = whole16(high)
    ref[*slot, extra(at), :] = whole16(packed - 32768.0)
    return power


def decode(ref, at, power, *slot):
    packed = wide(ref[*slot, extra(at), :]) + 32768.0
    digits = [jnp.floor(packed * 0.25**k) for k in range(8)]
    low = jnp.concatenate(
        [d - 4.0 * above for d, above in zip(digits, digits[1:] + [jnp.zeros_like(packed)])], axis=0
    )
    return (wide(ref[*slot, matrix(at), :]) * 4.0 + low) * jnp.exp2(power / 8.0 - 17.0)


def decode_high(ref, at, power, *slot):
    return wide(ref[*slot, matrix(at), :]) * jnp.exp2(power / 8.0 - 15.0)


def encode2(x):
    power = jnp.ceil(jnp.log2(jnp.maximum(jnp.abs(x), 1e-30)))
    scaled = x * jnp.exp2(14.0 - power)
    high = jnp.floor(scaled + 0.5)
    return power, high, jnp.floor((scaled - high) * 16384.0 + 0.5)


def decode2(power, high, low):
    return (high + low / 16384.0) * jnp.exp2(power - 14.0)


def log_parts(log):
    coarse = jnp.floor(log * 256.0 + 0.5)
    return coarse, jnp.floor((log - coarse / 256.0) * 8388608.0 + 0.5)


def log_whole(coarse, fine):
    return coarse / 256.0 + fine / 8388608.0


def rows16(*rows):
    at = iota((TAIL, LANES), 0)
    total = jnp.zeros((TAIL, LANES), F32)
    for i, row in enumerate(rows):
        total = jnp.where(at == i, row, total)
    return whole16(total)


def doc_of(pos, offsets_ref):
    total = (pos >= offsets_ref[0, 0]).astype(jnp.int32)
    for i in range(1, DOCS):
        total = total + (pos >= offsets_ref[0, i]).astype(jnp.int32)
    return total


def place():
    return lax.axis_index("seg") * lax.axis_size("grp") + lax.axis_index("grp")


def decays(gates, bias, offsets_ref):
    heads, length = gates.shape
    first = place() * length
    same = iota((heads, heads), 0) == iota((heads, heads), 1)
    logits = gates.astype(F32) + jnp.sum(jnp.where(same, bias, 0.0), axis=1, keepdims=True)
    step = -(jnp.maximum(logits, 0.0) + jnp.log1p(jnp.exp(-jnp.abs(logits))))
    causal = iota((length, length), 0) >= iota((length, length), 1)
    cumulative = nt(causal.astype(F32), step, HIGHEST)
    doc = doc_of(first + iota((length, 1), 0), offsets_ref)
    doc_last = doc_of(first + length - 1, offsets_ref)
    before = jnp.where(first > 0, doc_of(first - 1, offsets_ref), -1)
    entry = jnp.exp(cumulative) * (doc == before).astype(F32)
    tail = jnp.exp(cumulative[length - 1 :, :] - cumulative) * (doc == doc_last).astype(F32)
    return first, logits, step, causal, cumulative, doc, entry, tail, doc_last == before


def fetch(refs, held, sems):
    parts = sems.shape[1]
    width = held.shape[2] // parts
    copies = [
        [
            pltpu.make_async_copy(
                ref.at[0, :, pl.ds(p * width, width)], held.at[i, :, pl.ds(p * width, width)], sems.at[i, p]
            )
            for i, ref in enumerate(refs)
        ]
        for p in range(parts)
    ]
    for group in copies:
        for copy in group:
            copy.start()
    return copies


def arrive(copies, head, heads):
    each = heads // len(copies)
    if head % each == 0:
        for copy in copies[head // each]:
            copy.wait()


def states_kernel(
    query_ref, key_ref, value_ref, dout_ref, gate_ref, bias_ref, offsets_ref,
    pay_ref, held, sems, gate_held, bias_held, offsets_held, small_sems, pay, pay_sems,
):
    heads = bias_ref.shape[1]
    small = [
        pltpu.make_async_copy(gate_ref.at[0], gate_held, small_sems.at[0]),
        pltpu.make_async_copy(bias_ref, bias_held, small_sems.at[1]),
        pltpu.make_async_copy(offsets_ref, offsets_held, small_sems.at[2]),
    ]
    for copy in small:
        copy.start()
    copies = fetch((query_ref, key_ref, value_ref, dout_ref), held, sems)
    for copy in small:
        copy.wait()
    _, _, _, _, cumulative, _, entry, tail, passes = decays(gate_held[...], bias_held[...], offsets_held)
    coarse, fine = log_parts(jnp.where(passes, jnp.maximum(cumulative[-1:, :], -120.0), -128.0))
    powers, sent = {}, []
    for h in range(heads):
        arrive(copies, h, heads)
        cols = matrix(h)
        one = slice(h, h + 1)
        slot, m = divmod(h, 2)
        for at, left, right, weight in ((m, 1, 2, tail[:, one]), (2 + m, 0, 3, entry[:, one] * SCALE)):
            own = tn2(held[left, :, cols], held[right, :, cols].astype(F32) * weight)
            powers[at] = encode(own, pay, at, slot)
        if m == 1:
            pay[slot, tail_of(pay), :] = rows16(
                *(powers[i] for i in range(4)),
                *(x[:, i : i + 1] for i in (h - 1, h) for x in (coarse, fine)),
            )
            sent.append(pltpu.make_async_copy(pay.at[slot], pay_ref.at[slot], pay_sems.at[slot]))
            sent[-1].start()
    for copy in sent:
        copy.wait()


def chunk_logs(tails, m):
    return [log_whole(t[4 + 2 * m : 5 + 2 * m], t[5 + 2 * m : 6 + 2 * m]) for t in tails]


def totals_kernel(pay_ref, _, *send_refs):
    count = pay_ref.shape[0]
    tails = [wide(pay_ref[c, tail_of(pay_ref), :]) for c in range(count)]
    mine, segments = lax.axis_index("seg"), lax.axis_size("seg")
    at = iota((8, LANES), 0)
    logs = jnp.zeros((8, LANES), F32)
    for m in range(2):
        log = chunk_logs(tails, m)
        logs = jnp.where(at == m, sum(log), logs)
        ends = []
        for where, order in ((m, range(count)), (2 + m, range(count - 1, -1, -1))):
            carry = jnp.zeros((HEAD_DIM, HEAD_DIM), F32)
            for c in order:
                carry = jnp.exp(log[c]) * carry + decode(pay_ref, where, tails[c][where : where + 1], c)
            ends.append(carry)
        for distance, send_ref in enumerate(send_refs, 1):
            send_ref[matrix(m), :] = jnp.where(mine + distance < segments, *ends)
    for send_ref in send_refs:
        send_ref[pl.ds(2 * HEAD_DIM, 8), :] = logs


def scan_kernel(pay_ref, *refs):
    *got_refs, out_ref, held = refs
    count = pay_ref.shape[0]
    mine = lax.axis_index("seg")
    tails = [wide(pay_ref[c, tail_of(pay_ref), :]) for c in range(count)]
    at = iota((2 * count, LANES), 0)
    flows = jnp.zeros((2 * count, LANES), F32)
    powers = [[None] * 4 for _ in range(count)]
    for m in range(2):
        log = chunk_logs(tails, m)
        sent = [(jnp.exp(ref[pl.ds(2 * HEAD_DIM + m, 1), :]), ref[matrix(m), :]) for ref in got_refs]
        state = jnp.zeros((HEAD_DIM, HEAD_DIM), F32)
        for d in range(len(sent), 0, -1):
            state = jnp.where(mine >= d, sent[d - 1][0] * state + sent[d - 1][1], state)
        grad = jnp.zeros((HEAD_DIM, HEAD_DIM), F32)
        for d in range(1, len(sent) + 1):
            grad = jnp.where(mine < d, sent[d - 1][0] * grad + sent[d - 1][1], grad)
        for where, carry, order in ((m, state, range(count)), (2 + m, grad, range(count - 1, -1, -1))):
            for i, c in enumerate(order):
                powers[c][where] = encode(carry, out_ref, where, c)
                passing = jnp.exp(log[c])
                if where == m:
                    held[c] = carry
                else:
                    flow = passing * jnp.sum(held[c] * carry, axis=0, keepdims=True)
                    flows = jnp.where(at == 2 * c + m, flow, flows)
                if i < count - 1:
                    carry = passing * carry + decode(pay_ref, where, tails[c][where : where + 1], c)
    parts = encode2(jnp.sum(flows, axis=1, keepdims=True))
    for c in range(count):
        out_ref[c, tail_of(out_ref), :] = rows16(
            *powers[c], *(part[2 * c + m : 2 * c + m + 1] for m in range(2) for part in parts)
        )


def local_kernel(
    query_ref, key_ref, value_ref, dout_ref, gate_ref, bias_ref, offsets_ref,
    dq_ref, dk_ref, dv_ref, rows_ref, cols_ref, held, sems,
):
    heads, length = gate_ref.shape[1:]
    copies = fetch((query_ref, key_ref, value_ref, dout_ref), held, sems)
    first, logits, step, causal, cumulative, doc, entry, tail, passes = decays(
        gate_ref[0], bias_ref[...], offsets_ref
    )
    cumulative_row = nt(step, causal.astype(F32), HIGHEST)
    linked = causal & (doc == doc_of(first + iota((1, length), 1), offsets_ref))
    lane = iota((length, heads), 1)
    sublane = iota((heads, length), 0)
    ends = jnp.zeros((length, heads), F32)
    ends_row = jnp.zeros((heads, length), F32)
    for h in range(heads):
        arrive(copies, h, heads)
        cols = matrix(h)
        q, k, v, d = (held[i, :, cols] for i in range(4))
        weights = jnp.where(
            linked,
            jnp.exp(jnp.where(linked, cumulative[:, h : h + 1] - cumulative_row[h : h + 1, :], 0.0)),
            0.0,
        ) * SCALE
        probs = nt(q, k) * weights
        dprobs = nt(d, v)
        pairs = probs * dprobs
        probs = probs.astype(BF16)
        dscores = (dprobs * weights).astype(BF16)
        dq_ref[:, cols] = nn(dscores, k)
        dk_ref[:, cols] = tn(dscores, q)
        dv_ref[:, cols] = tn(probs, d)
        ends = jnp.where(lane == h, jnp.sum(pairs, axis=1, keepdims=True), ends)
        ends_row = jnp.where(sublane == h, jnp.sum(pairs, axis=0, keepdims=True), ends_row)
    causal = causal.astype(F32)
    rows_ref[0] = tn(ends, causal, HIGHEST) - nn(ends_row, causal, HIGHEST)
    rows_ref[1] = -1.0 / (1.0 + jnp.exp(-logits))
    cols_ref[0] = entry * SCALE
    cols_ref[1] = tail


def received(state_ref, head, decode):
    slot, m = divmod(head, 2)
    tail = wide(state_ref[slot, tail_of(state_ref), :])
    pair = tuple(decode(state_ref, i, tail[i : i + 1], slot) for i in (m, 2 + m))
    return *pair, decode2(*(tail[i : i + 1, :1] for i in range(4 + 3 * m, 7 + 3 * m)))


def gates_kernel(
    query_ref, key_ref, value_ref, dout_ref, rows_ref, cols_ref, state_ref, dgate_ref, dbias_ref
):
    heads, length = dgate_ref.shape[1:]
    lane = iota((length, heads), 1)
    sublane = iota((heads, 1), 0)
    ends = jnp.zeros((length, heads), F32)
    starts = jnp.zeros((length, heads), F32)
    flows = jnp.zeros((heads, 1), F32)
    for h in range(heads):
        state32, grad32, flow = received(state_ref, h, decode)
        q, k, v, d = (ref[0, :, matrix(h)] for ref in (query_ref, key_ref, value_ref, dout_ref))
        at_end = jnp.sum(q.astype(F32) * nt2(d, state32), axis=1, keepdims=True)
        at_start = jnp.sum(k.astype(F32) * nt2(v, grad32), axis=1, keepdims=True)
        ends = jnp.where(lane == h, at_end, ends)
        starts = jnp.where(lane == h, at_start, starts)
        flows = jnp.where(sublane == h, flow, flows)
    behind = iota((length, length), 0) - iota((length, length), 1)
    dstep = (
        rows_ref[0]
        + tn(ends * cols_ref[0], (behind >= 0).astype(F32), HIGHEST)
        + tn(starts * cols_ref[1], (behind < 0).astype(F32), HIGHEST)
        + flows
    )
    dlogit = dstep * rows_ref[1]
    dgate_ref[0] = dlogit.astype(BF16)
    same = iota((heads, heads), 0) == iota((heads, heads), 1)
    total = jnp.sum(jnp.where(same, jnp.sum(dlogit, axis=1, keepdims=True), 0.0), axis=0, keepdims=True)
    dbias_ref[...] = jnp.broadcast_to(total[None], dbias_ref.shape)


def output_kernel(
    key_ref, value_ref, dout_ref, cols_ref, state_ref, dq_near_ref, dk_near_ref, dv_near_ref,
    dq_ref, dk_ref, dv_ref,
):
    for h in range(cols_ref.shape[2]):
        cols = matrix(h)
        entry, tail = (cols_ref[i, :, h : h + 1] for i in range(2))
        state, grad = (x.astype(BF16) for x in received(state_ref, h, decode_high)[:2])
        for near_ref, out_ref, far, decay in (
            (dq_near_ref, dq_ref, nt(dout_ref[0, :, cols], state), entry),
            (dk_near_ref, dk_ref, nt(value_ref[0, :, cols], grad), tail),
            (dv_near_ref, dv_ref, nn(key_ref[0, :, cols], grad), tail),
        ):
            out_ref[0, :, cols] = (near_ref[:, cols] + decay * far).astype(BF16)


def call(kernel, out_shape, in_specs, **more):
    more.setdefault("out_specs", (VMEM,) * len(out_shape) if isinstance(out_shape, tuple) else VMEM)
    return pl.pallas_call(
        kernel, out_shape=out_shape, in_specs=in_specs, compiler_params=PARAMS, **more
    )


def shards(query, key, value, dout, gate_in, gate_bias, offsets):
    heads = gate_bias.shape[0]
    length, width = query.shape[1:]
    count, segments = lax.axis_size("grp"), lax.axis_size("seg")
    gates = jnp.swapaxes(gate_in, 1, 2)
    small = (gates, gate_bias.reshape(1, heads), offsets)
    pin = lambda xs: tuple(pltpu.with_memory_space_constraint(x, pltpu.HBM) for x in xs)
    big = pin((query, key, value, dout))
    scratch = [pltpu.VMEM((4, length, width), BF16), pltpu.SemaphoreType.DMA((4, 8))]
    packed = jax.ShapeDtypeStruct((count, SLOT, LANES), I16)
    pay = call(
        states_kernel,
        packed,
        [HBM] * 7,
        scratch_shapes=scratch
        + [
            pltpu.VMEM((heads, length), BF16),
            pltpu.VMEM((1, heads), F32),
            pltpu.SMEM(offsets.shape, jnp.int32),
            pltpu.SemaphoreType.DMA((3,)),
            pltpu.VMEM(packed.shape, I16),
            pltpu.SemaphoreType.DMA((count,)),
        ],
        out_specs=HBM,
    )(*big, *pin(small))
    pay = lax.all_to_all(pay, "grp", split_axis=0, concat_axis=0, tiled=True)
    near_like = jax.ShapeDtypeStruct((length, width), F32)
    *near, rows, cols = call(
        local_kernel,
        (near_like,) * 3
        + (jax.ShapeDtypeStruct((2, heads, length), F32), jax.ShapeDtypeStruct((2, length, heads), F32)),
        [HBM] * 4 + [VMEM] * 2 + [SMEM],
        scratch_shapes=scratch,
    )(*big, *small)
    total = jax.ShapeDtypeStruct((2 * HEAD_DIM + 8, LANES), F32)
    sends = call(totals_kernel, (total,) * (segments - 1), [VMEM, pl.BlockSpec(memory_space=pl.ANY)])(pay, rows)
    got = [
        lax.ppermute(send, "seg", [(i, (i + d) % segments) for i in range(segments)])
        for d, send in enumerate(sends, 1)
    ]
    carried = call(
        scan_kernel,
        packed,
        [VMEM] * segments,
        scratch_shapes=[pltpu.VMEM((count, HEAD_DIM, LANES), F32)],
    )(pay, *got)
    carried = lax.all_to_all(carried, "grp", split_axis=0, concat_axis=0, tiled=True)
    dgate, dbias = call(
        gates_kernel,
        (
            jax.ShapeDtypeStruct(gates.shape, BF16),
            jax.ShapeDtypeStruct((lax.axis_size(ALL), 1, heads), F32),
        ),
        [VMEM] * 7,
    )(query, key, value, dout, rows, cols, carried)
    everywhere = lax.all_to_all(dbias, ALL, split_axis=0, concat_axis=0, tiled=True)
    like = jax.ShapeDtypeStruct(query.shape, BF16)
    dq, dk, dv = call(output_kernel, (like,) * 3, [VMEM] * 8)(key, value, dout, cols, carried, *near)
    return dq, dk, dv, jnp.swapaxes(dgate, 1, 2), jnp.sum(everywhere, axis=(0, 1))


def solution(mesh):
    rows = P("dp", LINE, None)
    return jax.shard_map(
        shards,
        mesh=mesh,
        in_specs=(rows, rows, rows, rows, rows, P(), P("dp", None)),
        out_specs=(rows, rows, rows, rows, P()),
        check_vma=False,
    )
```

```python
import functools

import jax
import jax.numpy as jnp
from jax import lax
from jax.experimental import pallas as pl
from jax.experimental.pallas import tpu as pltpu
from jax.sharding import PartitionSpec as P

HEAD_DIM = 128
SCALE = HEAD_DIM ** (-0.5)
DOCS = 4
LINE = ("seg", "grp")
ALL = ("dp", "seg", "grp")
TAIL = 16
LANES = 128
F32 = jnp.float32
BF16 = jnp.bfloat16
I16 = jnp.int16
VMEM = pl.BlockSpec(memory_space=pltpu.VMEM)
SMEM = pl.BlockSpec(memory_space=pltpu.SMEM)
HBM = pl.BlockSpec(memory_space=pltpu.HBM)
HIGHEST = lax.Precision.HIGHEST
PARAMS = pltpu.CompilerParams(vmem_limit_bytes=20 * 1024 * 1024)


def dot(a, b, over, precision=None):
    return lax.dot_general(
        a, b, (((over[0],), (over[1],)), ((), ())), precision=precision, preferred_element_type=F32
    )


def nn(a, b, precision=None):
    return dot(a, b, (1, 0), precision)


def nt(a, b, precision=None):
    return dot(a, b, (1, 1), precision)


def tn(a, b, precision=None):
    return dot(a, b, (0, 0), precision)


def split2(x):
    hi = x.astype(BF16)
    return hi, (x - hi.astype(F32)).astype(BF16)


def tn2(a, b):
    both = tn(a, jnp.concatenate(split2(b), axis=1))
    return both[:, : b.shape[1]] + both[:, b.shape[1] :]


def nt2(a, b):
    both = nt(a, jnp.concatenate(split2(b), axis=0))
    return both[:, : b.shape[0]] + both[:, b.shape[0] :]


def matrix(m):
    return pl.ds(m * HEAD_DIM, HEAD_DIM)


def tail_of(ref):
    return pl.ds(ref.shape[-2] - TAIL, TAIL)


def iota(shape, dim):
    return lax.broadcasted_iota(jnp.int32, shape, dim)


def whole16(x):
    return x.astype(jnp.int32).astype(I16)


def wide(x):
    return x.astype(jnp.int32).astype(F32)


def encode(x):
    top = jnp.maximum(jnp.max(jnp.abs(x), axis=0, keepdims=True), 1e-30)
    power = jnp.ceil(jnp.log2(top) * 8.0)
    return jnp.clip(jnp.floor(x * jnp.exp2(15.0 - power / 8.0) + 0.5), -32767.0, 32767.0), power


def decode(steps, power):
    return wide(steps) * jnp.exp2(power / 8.0 - 15.0)


def encode2(x):
    power = jnp.ceil(jnp.log2(jnp.maximum(jnp.abs(x), 1e-30)))
    scaled = x * jnp.exp2(14.0 - power)
    high = jnp.floor(scaled + 0.5)
    return power, high, jnp.floor((scaled - high) * 16384.0 + 0.5)


def decode2(power, high, low):
    return (high + low / 16384.0) * jnp.exp2(power - 14.0)


def log_parts(log):
    coarse = jnp.floor(log * 256.0 + 0.5)
    return coarse, jnp.floor((log - coarse / 256.0) * 8388608.0 + 0.5)


def log_whole(coarse, fine):
    return coarse / 256.0 + fine / 8388608.0


def rows16(*rows):
    at = iota((TAIL, LANES), 0)
    total = jnp.zeros((TAIL, LANES), F32)
    for i, row in enumerate(rows):
        total = jnp.where(at == i, row, total)
    return whole16(total)


def doc_of(pos, offsets_ref):
    total = (pos >= offsets_ref[0, 0]).astype(jnp.int32)
    for i in range(1, DOCS):
        total = total + (pos >= offsets_ref[0, i]).astype(jnp.int32)
    return total


def place():
    return lax.axis_index("seg") * lax.axis_size("grp") + lax.axis_index("grp")


def spread(whole, *piece_refs):
    count, mine = lax.axis_size("grp"), lax.axis_index("grp")
    for d, ref in enumerate(piece_refs):
        ref[...] = whole[lax.rem(mine + d, count)]


def gather(whole, *piece_refs):
    count, mine = lax.axis_size("grp"), lax.axis_index("grp")
    for d, ref in enumerate(piece_refs):
        whole[lax.rem(mine + count - d, count)] = ref[...]


def exchange(pieces):
    count = len(pieces)
    got = {0: pieces[0]}
    for d in sorted(range(1, count), key=lambda d: (-min(d, count - d), d)):
        got[d] = lax.ppermute(pieces[d], "grp", [(i, (i + d) % count) for i in range(count)])
    return [got[d] for d in range(count)]


def decays(gates, bias, offsets_ref):
    heads, length = gates.shape
    first = place() * length
    same = iota((heads, heads), 0) == iota((heads, heads), 1)
    logits = gates.astype(F32) + jnp.sum(jnp.where(same, bias, 0.0), axis=1, keepdims=True)
    step = -(jnp.maximum(logits, 0.0) + jnp.log1p(jnp.exp(-jnp.abs(logits))))
    causal = iota((length, length), 0) >= iota((length, length), 1)
    cumulative = nt(causal.astype(F32), step, HIGHEST)
    doc = doc_of(first + iota((length, 1), 0), offsets_ref)
    doc_last = doc_of(first + length - 1, offsets_ref)
    before = jnp.where(first > 0, doc_of(first - 1, offsets_ref), -1)
    entry = jnp.exp(cumulative) * (doc == before).astype(F32)
    tail = jnp.exp(cumulative[length - 1 :, :] - cumulative) * (doc == doc_last).astype(F32)
    return first, logits, step, causal, cumulative, doc, entry, tail, doc_last == before


def fetch(refs, held, sems):
    parts = sems.shape[1]
    width = held.shape[2] // parts
    copies = [
        [
            pltpu.make_async_copy(
                ref.at[0, :, pl.ds(p * width, width)], held.at[i, :, pl.ds(p * width, width)], sems.at[i, p]
            )
            for i, ref in enumerate(refs)
        ]
        for p in range(parts)
    ]
    for group in copies:
        for copy in group:
            copy.start()
    return copies


def arrive(copies, head, heads):
    each = heads // len(copies)
    if head % each == 0:
        for copy in copies[head // each]:
            copy.wait()


def states_kernel(
    query_ref, key_ref, value_ref, dout_ref, gate_ref, bias_ref, offsets_ref, *refs
):
    *piece_refs, held, sems, gate_held, bias_held, offsets_held, small_sems, pay = refs
    heads = bias_ref.shape[1]
    small = [
        pltpu.make_async_copy(gate_ref.at[0], gate_held, small_sems.at[0]),
        pltpu.make_async_copy(bias_ref, bias_held, small_sems.at[1]),
        pltpu.make_async_copy(offsets_ref, offsets_held, small_sems.at[2]),
    ]
    for copy in small:
        copy.start()
    copies = fetch((query_ref, key_ref, value_ref, dout_ref), held, sems)
    for copy in small:
        copy.wait()
    _, _, _, _, cumulative, _, entry, tail, passes = decays(gate_held[...], bias_held[...], offsets_held)
    coarse, fine = log_parts(jnp.where(passes, jnp.maximum(cumulative[-1:, :], -120.0), -128.0))
    powers = {}
    for h in range(heads):
        arrive(copies, h, heads)
        cols = matrix(h)
        one = slice(h, h + 1)
        slot, m = divmod(h, 2)
        for at, left, right, weight in ((m, 1, 2, tail[:, one]), (2 + m, 0, 3, entry[:, one] * SCALE)):
            own = tn2(held[left, :, cols], held[right, :, cols].astype(F32) * weight)
            steps, powers[at] = encode(own)
            pay[slot, matrix(at), :] = whole16(steps)
        if m == 1:
            pay[slot, tail_of(pay), :] = rows16(
                *(powers[i] for i in range(4)),
                *(x[:, i : i + 1] for i in (h - 1, h) for x in (coarse, fine)),
            )
    spread(pay, *piece_refs)


def chunk_logs(tails, m):
    return [log_whole(t[4 + 2 * m : 5 + 2 * m], t[5 + 2 * m : 6 + 2 * m]) for t in tails]


def totals_kernel(count, *refs):
    piece_refs, (pay_ref, *send_refs) = refs[:count], refs[count + 1 :]
    gather(pay_ref, *piece_refs)
    tails = [wide(pay_ref[c, tail_of(pay_ref), :]) for c in range(count)]
    mine, segments = lax.axis_index("seg"), lax.axis_size("seg")
    at = iota((8, LANES), 0)
    logs = jnp.zeros((8, LANES), F32)
    for m in range(2):
        log = chunk_logs(tails, m)
        logs = jnp.where(at == m, sum(log), logs)
        ends = []
        for where, order in ((m, range(count)), (2 + m, range(count - 1, -1, -1))):
            carry = jnp.zeros((HEAD_DIM, HEAD_DIM), F32)
            for c in order:
                carry = jnp.exp(log[c]) * carry + decode(
                    pay_ref[c, matrix(where), :], tails[c][where : where + 1]
                )
            ends.append(carry)
        for distance, send_ref in enumerate(send_refs, 1):
            send_ref[matrix(m), :] = jnp.where(mine + distance < segments, *ends)
    for send_ref in send_refs:
        send_ref[pl.ds(2 * HEAD_DIM, 8), :] = logs


def scan_kernel(segments, pay_ref, *refs):
    got_refs, (*piece_refs, out_ref, held) = refs[: segments - 1], refs[segments - 1 :]
    count = pay_ref.shape[0]
    mine = lax.axis_index("seg")
    tails = [wide(pay_ref[c, tail_of(pay_ref), :]) for c in range(count)]
    at = iota((2 * count, LANES), 0)
    flows = jnp.zeros((2 * count, LANES), F32)
    powers = [[None] * 4 for _ in range(count)]
    for m in range(2):
        log = chunk_logs(tails, m)
        sent = [(jnp.exp(ref[pl.ds(2 * HEAD_DIM + m, 1), :]), ref[matrix(m), :]) for ref in got_refs]
        state = jnp.zeros((HEAD_DIM, HEAD_DIM), F32)
        for d in range(len(sent), 0, -1):
            state = jnp.where(mine >= d, sent[d - 1][0] * state + sent[d - 1][1], state)
        grad = jnp.zeros((HEAD_DIM, HEAD_DIM), F32)
        for d in range(1, len(sent) + 1):
            grad = jnp.where(mine < d, sent[d - 1][0] * grad + sent[d - 1][1], grad)
        for where, carry, order in ((m, state, range(count)), (2 + m, grad, range(count - 1, -1, -1))):
            for i, c in enumerate(order):
                steps, powers[c][where] = encode(carry)
                out_ref[c, matrix(where), :] = whole16(steps)
                passing = jnp.exp(log[c])
                if where == m:
                    held[c] = carry
                else:
                    flow = passing * jnp.sum(held[c] * carry, axis=0, keepdims=True)
                    flows = jnp.where(at == 2 * c + m, flow, flows)
                if i < count - 1:
                    carry = passing * carry + decode(pay_ref[c, matrix(where), :], tails[c][where : where + 1])
    parts = encode2(jnp.sum(flows, axis=1, keepdims=True))
    for c in range(count):
        out_ref[c, tail_of(out_ref), :] = rows16(
            *powers[c], *(part[2 * c + m : 2 * c + m + 1] for m in range(2) for part in parts)
        )
    spread(out_ref, *piece_refs)


def local_kernel(
    query_ref, key_ref, value_ref, dout_ref, gate_ref, bias_ref, offsets_ref,
    dq_ref, dk_ref, dv_ref, rows_ref, cols_ref, held, sems,
):
    heads, length = gate_ref.shape[1:]
    copies = fetch((query_ref, key_ref, value_ref, dout_ref), held, sems)
    first, logits, step, causal, cumulative, doc, entry, tail, passes = decays(
        gate_ref[0], bias_ref[...], offsets_ref
    )
    cumulative_row = nt(step, causal.astype(F32), HIGHEST)
    linked = causal & (doc == doc_of(first + iota((1, length), 1), offsets_ref))
    lane = iota((length, heads), 1)
    sublane = iota((heads, length), 0)
    ends = jnp.zeros((length, heads), F32)
    ends_row = jnp.zeros((heads, length), F32)
    for h in range(heads):
        arrive(copies, h, heads)
        cols = matrix(h)
        q, k, v, d = (held[i, :, cols] for i in range(4))
        weights = jnp.where(
            linked,
            jnp.exp(jnp.where(linked, cumulative[:, h : h + 1] - cumulative_row[h : h + 1, :], 0.0)),
            0.0,
        ) * SCALE
        probs = nt(q, k) * weights
        dprobs = nt(d, v)
        pairs = probs * dprobs
        probs = probs.astype(BF16)
        dscores = (dprobs * weights).astype(BF16)
        dq_ref[:, cols] = nn(dscores, k)
        dk_ref[:, cols] = tn(dscores, q)
        dv_ref[:, cols] = tn(probs, d)
        ends = jnp.where(lane == h, jnp.sum(pairs, axis=1, keepdims=True), ends)
        ends_row = jnp.where(sublane == h, jnp.sum(pairs, axis=0, keepdims=True), ends_row)
    causal = causal.astype(F32)
    rows_ref[0] = tn(ends, causal, HIGHEST) - nn(ends_row, causal, HIGHEST)
    rows_ref[1] = -1.0 / (1.0 + jnp.exp(-logits))
    cols_ref[0] = entry * SCALE
    cols_ref[1] = tail


def received(state_ref, head):
    slot, m = divmod(head, 2)
    tail = wide(state_ref[slot, tail_of(state_ref), :])
    pair = tuple(decode(state_ref[slot, matrix(i), :], tail[i : i + 1]) for i in (m, 2 + m))
    return *pair, decode2(*(tail[i : i + 1, :1] for i in range(4 + 3 * m, 7 + 3 * m)))


def gates_kernel(query_ref, key_ref, value_ref, dout_ref, rows_ref, cols_ref, *refs):
    *piece_refs, dgate_ref, dbias_ref, state_ref = refs
    gather(state_ref, *piece_refs)
    heads, length = dgate_ref.shape[1:]
    lane = iota((length, heads), 1)
    sublane = iota((heads, 1), 0)
    ends = jnp.zeros((length, heads), F32)
    starts = jnp.zeros((length, heads), F32)
    flows = jnp.zeros((heads, 1), F32)
    for h in range(heads):
        state32, grad32, flow = received(state_ref, h)
        q, k, v, d = (ref[0, :, matrix(h)] for ref in (query_ref, key_ref, value_ref, dout_ref))
        at_end = jnp.sum(q.astype(F32) * nt2(d, state32), axis=1, keepdims=True)
        at_start = jnp.sum(k.astype(F32) * nt2(v, grad32), axis=1, keepdims=True)
        ends = jnp.where(lane == h, at_end, ends)
        starts = jnp.where(lane == h, at_start, starts)
        flows = jnp.where(sublane == h, flow, flows)
    behind = iota((length, length), 0) - iota((length, length), 1)
    dstep = (
        rows_ref[0]
        + tn(ends * cols_ref[0], (behind >= 0).astype(F32), HIGHEST)
        + tn(starts * cols_ref[1], (behind < 0).astype(F32), HIGHEST)
        + flows
    )
    dlogit = dstep * rows_ref[1]
    dgate_ref[0] = dlogit.astype(BF16)
    same = iota((heads, heads), 0) == iota((heads, heads), 1)
    total = jnp.sum(jnp.where(same, jnp.sum(dlogit, axis=1, keepdims=True), 0.0), axis=0, keepdims=True)
    dbias_ref[...] = jnp.broadcast_to(total[None], dbias_ref.shape)


def output_kernel(
    key_ref, value_ref, dout_ref, cols_ref, dq_near_ref, dk_near_ref, dv_near_ref, *refs
):
    *piece_refs, dq_ref, dk_ref, dv_ref, state_ref = refs
    gather(state_ref, *piece_refs)
    for h in range(cols_ref.shape[2]):
        cols = matrix(h)
        entry, tail = (cols_ref[i, :, h : h + 1] for i in range(2))
        state, grad = (x.astype(BF16) for x in received(state_ref, h)[:2])
        for near_ref, out_ref, far, decay in (
            (dq_near_ref, dq_ref, nt(dout_ref[0, :, cols], state), entry),
            (dk_near_ref, dk_ref, nt(value_ref[0, :, cols], grad), tail),
            (dv_near_ref, dv_ref, nn(key_ref[0, :, cols], grad), tail),
        ):
            out_ref[0, :, cols] = (near_ref[:, cols] + decay * far).astype(BF16)


def call(kernel, out_shape, in_specs, **more):
    more.setdefault("out_specs", (VMEM,) * len(out_shape) if isinstance(out_shape, tuple) else VMEM)
    return pl.pallas_call(
        kernel, out_shape=out_shape, in_specs=in_specs, compiler_params=PARAMS, **more
    )


def shards(query, key, value, dout, gate_in, gate_bias, offsets):
    heads = gate_bias.shape[0]
    length, width = query.shape[1:]
    count, segments = lax.axis_size("grp"), lax.axis_size("seg")
    gates = jnp.swapaxes(gate_in, 1, 2)
    small = (gates, gate_bias.reshape(1, heads), offsets)
    pin = lambda xs: tuple(pltpu.with_memory_space_constraint(x, pltpu.HBM) for x in xs)
    big = pin((query, key, value, dout))
    scratch = [pltpu.VMEM((4, length, width), BF16), pltpu.SemaphoreType.DMA((4, 8))]
    piece = jax.ShapeDtypeStruct((4 * HEAD_DIM + TAIL, LANES), I16)
    packed = jax.ShapeDtypeStruct((count,) + piece.shape, I16)
    pieces = call(
        states_kernel,
        (piece,) * count,
        [HBM] * 7,
        scratch_shapes=scratch
        + [
            pltpu.VMEM((heads, length), BF16),
            pltpu.VMEM((1, heads), F32),
            pltpu.SMEM(offsets.shape, jnp.int32),
            pltpu.SemaphoreType.DMA((3,)),
            pltpu.VMEM(packed.shape, I16),
        ],
    )(*big, *pin(small))
    pieces = exchange(pieces)
    near_like = jax.ShapeDtypeStruct((length, width), F32)
    *near, rows, cols = call(
        local_kernel,
        (near_like,) * 3
        + (jax.ShapeDtypeStruct((2, heads, length), F32), jax.ShapeDtypeStruct((2, length, heads), F32)),
        [HBM] * 4 + [VMEM] * 2 + [SMEM],
        scratch_shapes=scratch,
    )(*big, *small)
    total = jax.ShapeDtypeStruct((2 * HEAD_DIM + 8, LANES), F32)
    pay, *sends = call(
        functools.partial(totals_kernel, count),
        (packed,) + (total,) * (segments - 1),
        [VMEM] * count + [pl.BlockSpec(memory_space=pl.ANY)],
    )(*pieces, rows)
    got = [
        lax.ppermute(send, "seg", [(i, (i + d) % segments) for i in range(segments)])
        for d, send in enumerate(sends, 1)
    ]
    carried = call(
        functools.partial(scan_kernel, segments),
        (piece,) * count,
        [VMEM] * segments,
        scratch_shapes=[pltpu.VMEM(packed.shape, I16), pltpu.VMEM((count, HEAD_DIM, LANES), F32)],
    )(pay, *got)
    carried = exchange(carried)
    assembled = [pltpu.VMEM(packed.shape, I16)]
    dgate, dbias = call(
        gates_kernel,
        (
            jax.ShapeDtypeStruct(gates.shape, BF16),
            jax.ShapeDtypeStruct((lax.axis_size(ALL), 1, heads), F32),
        ),
        [VMEM] * (6 + count),
        scratch_shapes=assembled,
    )(query, key, value, dout, rows, cols, *carried)
    everywhere = lax.all_to_all(dbias, ALL, split_axis=0, concat_axis=0, tiled=True)
    like = jax.ShapeDtypeStruct(query.shape, BF16)
    dq, dk, dv = call(output_kernel, (like,) * 3, [VMEM] * (7 + count), scratch_shapes=assembled)(
        key, value, dout, cols, *near, *carried
    )
    return dq, dk, dv, jnp.swapaxes(dgate, 1, 2), jnp.sum(everywhere, axis=(0, 1))


def solution(mesh):
    rows = P("dp", LINE, None)
    return jax.shard_map(
        shards,
        mesh=mesh,
        in_specs=(rows, rows, rows, rows, rows, P(), P("dp", None)),
        out_specs=(rows, rows, rows, rows, P()),
        check_vma=False,
    )
```

```python
import jax
import jax.numpy as jnp
from jax import lax
from jax.experimental import pallas as pl
from jax.experimental.pallas import tpu as pltpu
from jax.sharding import PartitionSpec as P

HEAD_DIM = 128
SCALE = HEAD_DIM ** (-0.5)
DOCS = 4
LINE = ("seg", "grp")
ALL = ("dp", "seg", "grp")
TAIL = 16
LANES = 128
EXTRA = HEAD_DIM // 8
F32 = jnp.float32
BF16 = jnp.bfloat16
I16 = jnp.int16
VMEM = pl.BlockSpec(memory_space=pltpu.VMEM)
SMEM = pl.BlockSpec(memory_space=pltpu.SMEM)
HBM = pl.BlockSpec(memory_space=pltpu.HBM)
HIGHEST = lax.Precision.HIGHEST
PARAMS = pltpu.CompilerParams(vmem_limit_bytes=20 * 1024 * 1024)


def dot(a, b, over, precision=None):
    return lax.dot_general(
        a, b, (((over[0],), (over[1],)), ((), ())), precision=precision, preferred_element_type=F32
    )


def nn(a, b, precision=None):
    return dot(a, b, (1, 0), precision)


def nt(a, b, precision=None):
    return dot(a, b, (1, 1), precision)


def tn(a, b, precision=None):
    return dot(a, b, (0, 0), precision)


def split2(x):
    hi = x.astype(BF16)
    return hi, (x - hi.astype(F32)).astype(BF16)


def tn2(a, b):
    both = tn(a, jnp.concatenate(split2(b), axis=1))
    return both[:, : b.shape[1]] + both[:, b.shape[1] :]


def nt2(a, b):
    both = nt(a, jnp.concatenate(split2(b), axis=0))
    return both[:, : b.shape[0]] + both[:, b.shape[0] :]


def matrix(m):
    return pl.ds(m * HEAD_DIM, HEAD_DIM)


def tail_of(ref):
    return pl.ds(ref.shape[-2] - TAIL, TAIL)


def extra(m):
    return pl.ds(2 * HEAD_DIM + m * EXTRA, EXTRA)


def extra_in(m):
    return pl.ds(4 * HEAD_DIM + m * EXTRA, EXTRA)


def iota(shape, dim):
    return lax.broadcasted_iota(jnp.int32, shape, dim)


def whole16(x):
    return x.astype(jnp.int32).astype(I16)


def wide(x):
    return x.astype(jnp.int32).astype(F32)


def encode(x):
    top = jnp.maximum(jnp.max(jnp.abs(x), axis=0, keepdims=True), 1e-30)
    power = jnp.ceil(jnp.log2(top) * 8.0)
    return jnp.clip(jnp.floor(x * jnp.exp2(15.0 - power / 8.0) + 0.5), -32767.0, 32767.0), power


def decode(steps, power):
    return wide(steps) * jnp.exp2(power / 8.0 - 15.0)


def encode18(x):
    top = jnp.maximum(jnp.max(jnp.abs(x), axis=0, keepdims=True), 1e-30)
    power = jnp.ceil(jnp.log2(top) * 8.0)
    steps = jnp.clip(jnp.floor(x * jnp.exp2(17.0 - power / 8.0) + 0.5), -131071.0, 131071.0)
    high = jnp.floor(steps * 0.25)
    low = steps - 4.0 * high
    return high, sum(low[k * EXTRA : (k + 1) * EXTRA] * 4.0**k for k in range(8)) - 32768.0, power


def decode18(high, packed, power):
    packed = wide(packed) + 32768.0
    digits = [jnp.floor(packed * 0.25**k) for k in range(8)]
    low = jnp.concatenate(
        [d - 4.0 * above for d, above in zip(digits, digits[1:] + [jnp.zeros_like(packed)])], axis=0
    )
    return (wide(high) * 4.0 + low) * jnp.exp2(power / 8.0 - 17.0)


def encode2(x):
    power = jnp.ceil(jnp.log2(jnp.maximum(jnp.abs(x), 1e-30)))
    scaled = x * jnp.exp2(14.0 - power)
    high = jnp.floor(scaled + 0.5)
    return power, high, jnp.floor((scaled - high) * 16384.0 + 0.5)


def decode2(power, high, low):
    return (high + low / 16384.0) * jnp.exp2(power - 14.0)


def log_parts(log):
    coarse = jnp.floor(log * 256.0 + 0.5)
    return coarse, jnp.floor((log - coarse / 256.0) * 8388608.0 + 0.5)


def log_whole(coarse, fine):
    return coarse / 256.0 + fine / 8388608.0


def rows16(*rows):
    at = iota((TAIL, LANES), 0)
    total = jnp.zeros((TAIL, LANES), F32)
    for i, row in enumerate(rows):
        total = jnp.where(at == i, row, total)
    return whole16(total)


def doc_of(pos, offsets_ref):
    total = (pos >= offsets_ref[0, 0]).astype(jnp.int32)
    for i in range(1, DOCS):
        total = total + (pos >= offsets_ref[0, i]).astype(jnp.int32)
    return total


def place():
    return lax.axis_index("seg") * lax.axis_size("grp") + lax.axis_index("grp")


def decays(gates, bias, offsets_ref):
    heads, length = gates.shape
    first = place() * length
    same = iota((heads, heads), 0) == iota((heads, heads), 1)
    logits = gates.astype(F32) + jnp.sum(jnp.where(same, bias, 0.0), axis=1, keepdims=True)
    step = -(jnp.maximum(logits, 0.0) + jnp.log1p(jnp.exp(-jnp.abs(logits))))
    causal = iota((length, length), 0) >= iota((length, length), 1)
    cumulative = nt(causal.astype(F32), step, HIGHEST)
    doc = doc_of(first + iota((length, 1), 0), offsets_ref)
    doc_last = doc_of(first + length - 1, offsets_ref)
    before = jnp.where(first > 0, doc_of(first - 1, offsets_ref), -1)
    entry = jnp.exp(cumulative) * (doc == before).astype(F32)
    tail = jnp.exp(cumulative[length - 1 :, :] - cumulative) * (doc == doc_last).astype(F32)
    return first, logits, step, causal, cumulative, doc, entry, tail, doc_last == before


def fetch(refs, held, sems):
    parts = sems.shape[1]
    width = held.shape[2] // parts
    copies = [
        [
            pltpu.make_async_copy(
                ref.at[0, :, pl.ds(p * width, width)], held.at[i, :, pl.ds(p * width, width)], sems.at[i, p]
            )
            for i, ref in enumerate(refs)
        ]
        for p in range(parts)
    ]
    for group in copies:
        for copy in group:
            copy.start()
    return copies


def arrive(copies, head, heads):
    each = heads // len(copies)
    if head % each == 0:
        for copy in copies[head // each]:
            copy.wait()


def states_kernel(
    query_ref, key_ref, value_ref, dout_ref, gate_ref, bias_ref, offsets_ref,
    pay_ref, held, sems, gate_held, bias_held, offsets_held, small_sems, pay, pay_sems,
):
    heads = bias_ref.shape[1]
    small = [
        pltpu.make_async_copy(gate_ref.at[0], gate_held, small_sems.at[0]),
        pltpu.make_async_copy(bias_ref, bias_held, small_sems.at[1]),
        pltpu.make_async_copy(offsets_ref, offsets_held, small_sems.at[2]),
    ]
    for copy in small:
        copy.start()
    copies = fetch((query_ref, key_ref, value_ref, dout_ref), held, sems)
    for copy in small:
        copy.wait()
    _, _, _, _, cumulative, _, entry, tail, passes = decays(gate_held[...], bias_held[...], offsets_held)
    coarse, fine = log_parts(jnp.where(passes, jnp.maximum(cumulative[-1:, :], -120.0), -128.0))
    powers, sent = {}, []
    for h in range(heads):
        arrive(copies, h, heads)
        cols = matrix(h)
        one = slice(h, h + 1)
        slot, m = divmod(h, 2)
        for at, left, right, weight in ((m, 1, 2, tail[:, one]), (2 + m, 0, 3, entry[:, one] * SCALE)):
            own = tn2(held[left, :, cols], held[right, :, cols].astype(F32) * weight)
            high, low, powers[at] = encode18(own)
            pay[slot, matrix(at), :] = whole16(high)
            pay[slot, extra_in(at), :] = whole16(low)
        if m == 1:
            pay[slot, tail_of(pay), :] = rows16(
                *(powers[i] for i in range(4)),
                *(x[:, i : i + 1] for i in (h - 1, h) for x in (coarse, fine)),
            )
            sent.append(pltpu.make_async_copy(pay.at[slot], pay_ref.at[slot], pay_sems.at[slot]))
            sent[-1].start()
    for copy in sent:
        copy.wait()


def chunk_logs(tails, m):
    return [log_whole(t[4 + 2 * m : 5 + 2 * m], t[5 + 2 * m : 6 + 2 * m]) for t in tails]


def totals_kernel(pay_ref, _, own_ref, *send_refs):
    count = pay_ref.shape[0]
    tails = [wide(pay_ref[c, tail_of(pay_ref), :]) for c in range(count)]
    mine, segments = lax.axis_index("seg"), lax.axis_size("seg")
    powers, logs = [], []
    for m in range(2):
        log = chunk_logs(tails, m)
        logs.extend(log_parts(jnp.maximum(sum(log), -128.0)))
        ends = []
        for where, order in ((m, range(count)), (2 + m, range(count - 1, -1, -1))):
            carry = jnp.zeros((HEAD_DIM, HEAD_DIM), F32)
            for c in order:
                own = decode18(
                    pay_ref[c, matrix(where), :], pay_ref[c, extra_in(where), :], tails[c][where : where + 1]
                )
                own_ref[c, matrix(where), :] = own
                carry = jnp.exp(log[c]) * carry + own
            ends.append(encode18(carry))
        powers.append([end[2] for end in ends])
        for distance, send_ref in enumerate(send_refs, 1):
            later = mine + distance < segments
            send_ref[matrix(m), :] = whole16(jnp.where(later, ends[0][0], ends[1][0]))
            send_ref[extra(m), :] = whole16(jnp.where(later, ends[0][1], ends[1][1]))
    for distance, send_ref in enumerate(send_refs, 1):
        later = mine + distance < segments
        send_ref[tail_of(send_ref), :] = rows16(*(jnp.where(later, *pair) for pair in powers), *logs)


def scan_kernel(pay_ref, own_ref, *refs):
    *got_refs, out_ref, held = refs
    count = pay_ref.shape[0]
    mine = lax.axis_index("seg")
    tails = [wide(pay_ref[c, tail_of(pay_ref), :]) for c in range(count)]
    got_tails = [wide(ref[tail_of(ref), :]) for ref in got_refs]
    at = iota((2 * count, LANES), 0)
    flows = jnp.zeros((2 * count, LANES), F32)
    powers = [[None] * 4 for _ in range(count)]
    for m in range(2):
        log = chunk_logs(tails, m)
        sent = [
            (
                jnp.exp(log_whole(t[2 + 2 * m : 3 + 2 * m], t[3 + 2 * m : 4 + 2 * m])),
                decode18(ref[matrix(m), :], ref[extra(m), :], t[m : m + 1]),
            )
            for ref, t in zip(got_refs, got_tails)
        ]
        state = jnp.zeros((HEAD_DIM, HEAD_DIM), F32)
        for d in range(len(sent), 0, -1):
            state = jnp.where(mine >= d, sent[d - 1][0] * state + sent[d - 1][1], state)
        grad = jnp.zeros((HEAD_DIM, HEAD_DIM), F32)
        for d in range(1, len(sent) + 1):
            grad = jnp.where(mine < d, sent[d - 1][0] * grad + sent[d - 1][1], grad)
        for where, carry, order in ((m, state, range(count)), (2 + m, grad, range(count - 1, -1, -1))):
            for i, c in enumerate(order):
                steps, powers[c][where] = encode(carry)
                out_ref[c, matrix(where), :] = whole16(steps)
                passing = jnp.exp(log[c])
                if where == m:
                    held[c] = carry
                else:
                    flow = passing * jnp.sum(held[c] * carry, axis=0, keepdims=True)
                    flows = jnp.where(at == 2 * c + m, flow, flows)
                if i < count - 1:
                    carry = passing * carry + own_ref[c, matrix(where), :]
    parts = encode2(jnp.sum(flows, axis=1, keepdims=True))
    for c in range(count):
        out_ref[c, tail_of(out_ref), :] = rows16(
            *powers[c], *(part[2 * c + m : 2 * c + m + 1] for m in range(2) for part in parts)
        )


def local_kernel(
    query_ref, key_ref, value_ref, dout_ref, gate_ref, bias_ref, offsets_ref,
    dq_ref, dk_ref, dv_ref, rows_ref, cols_ref, held, sems,
):
    heads, length = gate_ref.shape[1:]
    copies = fetch((query_ref, key_ref, value_ref, dout_ref), held, sems)
    first, logits, step, causal, cumulative, doc, entry, tail, passes = decays(
        gate_ref[0], bias_ref[...], offsets_ref
    )
    cumulative_row = nt(step, causal.astype(F32), HIGHEST)
    linked = causal & (doc == doc_of(first + iota((1, length), 1), offsets_ref))
    lane = iota((length, heads), 1)
    sublane = iota((heads, length), 0)
    ends = jnp.zeros((length, heads), F32)
    ends_row = jnp.zeros((heads, length), F32)
    for h in range(heads):
        arrive(copies, h, heads)
        cols = matrix(h)
        q, k, v, d = (held[i, :, cols] for i in range(4))
        weights = jnp.where(
            linked,
            jnp.exp(jnp.where(linked, cumulative[:, h : h + 1] - cumulative_row[h : h + 1, :], 0.0)),
            0.0,
        ) * SCALE
        probs = nt(q, k) * weights
        dprobs = nt(d, v)
        pairs = probs * dprobs
        probs = probs.astype(BF16)
        dscores = (dprobs * weights).astype(BF16)
        dq_ref[:, cols] = nn(dscores, k)
        dk_ref[:, cols] = tn(dscores, q)
        dv_ref[:, cols] = tn(probs, d)
        ends = jnp.where(lane == h, jnp.sum(pairs, axis=1, keepdims=True), ends)
        ends_row = jnp.where(sublane == h, jnp.sum(pairs, axis=0, keepdims=True), ends_row)
    causal = causal.astype(F32)
    rows_ref[0] = tn(ends, causal, HIGHEST) - nn(ends_row, causal, HIGHEST)
    rows_ref[1] = -1.0 / (1.0 + jnp.exp(-logits))
    cols_ref[0] = entry * SCALE
    cols_ref[1] = tail


def received(state_ref, head):
    slot, m = divmod(head, 2)
    tail = wide(state_ref[slot, tail_of(state_ref), :])
    pair = tuple(decode(state_ref[slot, matrix(i), :], tail[i : i + 1]) for i in (m, 2 + m))
    return *pair, decode2(*(tail[i : i + 1, :1] for i in range(4 + 3 * m, 7 + 3 * m)))


def gates_kernel(
    query_ref, key_ref, value_ref, dout_ref, rows_ref, cols_ref, state_ref, dgate_ref, dbias_ref
):
    heads, length = dgate_ref.shape[1:]
    lane = iota((length, heads), 1)
    sublane = iota((heads, 1), 0)
    ends = jnp.zeros((length, heads), F32)
    starts = jnp.zeros((length, heads), F32)
    flows = jnp.zeros((heads, 1), F32)
    for h in range(heads):
        state32, grad32, flow = received(state_ref, h)
        q, k, v, d = (ref[0, :, matrix(h)] for ref in (query_ref, key_ref, value_ref, dout_ref))
        at_end = jnp.sum(q.astype(F32) * nt2(d, state32), axis=1, keepdims=True)
        at_start = jnp.sum(k.astype(F32) * nt2(v, grad32), axis=1, keepdims=True)
        ends = jnp.where(lane == h, at_end, ends)
        starts = jnp.where(lane == h, at_start, starts)
        flows = jnp.where(sublane == h, flow, flows)
    behind = iota((length, length), 0) - iota((length, length), 1)
    dstep = (
        rows_ref[0]
        + tn(ends * cols_ref[0], (behind >= 0).astype(F32), HIGHEST)
        + tn(starts * cols_ref[1], (behind < 0).astype(F32), HIGHEST)
        + flows
    )
    dlogit = dstep * rows_ref[1]
    dgate_ref[0] = dlogit.astype(BF16)
    same = iota((heads, heads), 0) == iota((heads, heads), 1)
    total = jnp.sum(jnp.where(same, jnp.sum(dlogit, axis=1, keepdims=True), 0.0), axis=0, keepdims=True)
    dbias_ref[...] = jnp.broadcast_to(total[None], dbias_ref.shape)


def output_kernel(
    key_ref, value_ref, dout_ref, cols_ref, state_ref, dq_near_ref, dk_near_ref, dv_near_ref,
    dq_ref, dk_ref, dv_ref,
):
    for h in range(cols_ref.shape[2]):
        cols = matrix(h)
        entry, tail = (cols_ref[i, :, h : h + 1] for i in range(2))
        state, grad = (x.astype(BF16) for x in received(state_ref, h)[:2])
        for near_ref, out_ref, far, decay in (
            (dq_near_ref, dq_ref, nt(dout_ref[0, :, cols], state), entry),
            (dk_near_ref, dk_ref, nt(value_ref[0, :, cols], grad), tail),
            (dv_near_ref, dv_ref, nn(key_ref[0, :, cols], grad), tail),
        ):
            out_ref[0, :, cols] = (near_ref[:, cols] + decay * far).astype(BF16)


def call(kernel, out_shape, in_specs, **more):
    more.setdefault("out_specs", (VMEM,) * len(out_shape) if isinstance(out_shape, tuple) else VMEM)
    return pl.pallas_call(
        kernel, out_shape=out_shape, in_specs=in_specs, compiler_params=PARAMS, **more
    )


def shards(query, key, value, dout, gate_in, gate_bias, offsets):
    heads = gate_bias.shape[0]
    length, width = query.shape[1:]
    count, segments = lax.axis_size("grp"), lax.axis_size("seg")
    gates = jnp.swapaxes(gate_in, 1, 2)
    small = (gates, gate_bias.reshape(1, heads), offsets)
    pin = lambda xs: tuple(pltpu.with_memory_space_constraint(x, pltpu.HBM) for x in xs)
    big = pin((query, key, value, dout))
    scratch = [pltpu.VMEM((4, length, width), BF16), pltpu.SemaphoreType.DMA((4, 8))]
    packed = jax.ShapeDtypeStruct((count, 4 * HEAD_DIM + TAIL, LANES), I16)
    packed_in = jax.ShapeDtypeStruct((count, 4 * (HEAD_DIM + EXTRA) + TAIL, LANES), I16)
    pay = call(
        states_kernel,
        packed_in,
        [HBM] * 7,
        scratch_shapes=scratch
        + [
            pltpu.VMEM((heads, length), BF16),
            pltpu.VMEM((1, heads), F32),
            pltpu.SMEM(offsets.shape, jnp.int32),
            pltpu.SemaphoreType.DMA((3,)),
            pltpu.VMEM(packed_in.shape, I16),
            pltpu.SemaphoreType.DMA((count,)),
        ],
        out_specs=HBM,
    )(*big, *pin(small))
    pay = lax.all_to_all(pay, "grp", split_axis=0, concat_axis=0, tiled=True)
    near_like = jax.ShapeDtypeStruct((length, width), F32)
    *near, rows, cols = call(
        local_kernel,
        (near_like,) * 3
        + (jax.ShapeDtypeStruct((2, heads, length), F32), jax.ShapeDtypeStruct((2, length, heads), F32)),
        [HBM] * 4 + [VMEM] * 2 + [SMEM],
        scratch_shapes=scratch,
    )(*big, *small)
    total = jax.ShapeDtypeStruct((2 * HEAD_DIM + 2 * EXTRA + TAIL, LANES), I16)
    own, *sends = call(
        totals_kernel,
        (jax.ShapeDtypeStruct((count, 4 * HEAD_DIM, LANES), F32),) + (total,) * (segments - 1),
        [VMEM, pl.BlockSpec(memory_space=pl.ANY)],
    )(pay, rows)
    got = {
        d: lax.ppermute(sends[d - 1], "seg", [(i, (i + d) % segments) for i in range(segments)])
        for d in sorted(range(1, segments), key=lambda d: -min(d, segments - d))
    }
    got = [got[d] for d in range(1, segments)]
    carried = call(
        scan_kernel,
        packed,
        [VMEM] * (segments + 1),
        scratch_shapes=[pltpu.VMEM((count, HEAD_DIM, LANES), F32)],
    )(pay, own, *got)
    carried = lax.all_to_all(carried, "grp", split_axis=0, concat_axis=0, tiled=True)
    dgate, dbias = call(
        gates_kernel,
        (
            jax.ShapeDtypeStruct(gates.shape, BF16),
            jax.ShapeDtypeStruct((lax.axis_size(ALL), 1, heads), F32),
        ),
        [VMEM] * 7,
    )(query, key, value, dout, rows, cols, carried)
    everywhere = lax.all_to_all(dbias, ALL, split_axis=0, concat_axis=0, tiled=True)
    like = jax.ShapeDtypeStruct(query.shape, BF16)
    dq, dk, dv = call(output_kernel, (like,) * 3, [VMEM] * 8)(key, value, dout, cols, carried, *near)
    return dq, dk, dv, jnp.swapaxes(dgate, 1, 2), jnp.sum(everywhere, axis=(0, 1))


def solution(mesh):
    rows = P("dp", LINE, None)
    return jax.shard_map(
        shards,
        mesh=mesh,
        in_specs=(rows, rows, rows, rows, rows, P(), P("dp", None)),
        out_specs=(rows, rows, rows, rows, P()),
        check_vma=False,
    )
```

```python
import jax
import jax.numpy as jnp
from jax import lax
from jax.experimental import pallas as pl
from jax.experimental.pallas import tpu as pltpu
from jax.sharding import PartitionSpec as P

HEAD_DIM = 128
SCALE = HEAD_DIM ** (-0.5)
DOCS = 4
LINE = ("seg", "grp")
ALL = ("dp", "seg", "grp")
TAIL = 16
LANES = 128
EXTRA = HEAD_DIM // 8
F32 = jnp.float32
BF16 = jnp.bfloat16
I16 = jnp.int16
VMEM = pl.BlockSpec(memory_space=pltpu.VMEM)
SMEM = pl.BlockSpec(memory_space=pltpu.SMEM)
HBM = pl.BlockSpec(memory_space=pltpu.HBM)
HIGHEST = lax.Precision.HIGHEST
PARAMS = pltpu.CompilerParams(vmem_limit_bytes=20 * 1024 * 1024)


def dot(a, b, over, precision=None):
    return lax.dot_general(
        a, b, (((over[0],), (over[1],)), ((), ())), precision=precision, preferred_element_type=F32
    )


def nn(a, b, precision=None):
    return dot(a, b, (1, 0), precision)


def nt(a, b, precision=None):
    return dot(a, b, (1, 1), precision)


def tn(a, b, precision=None):
    return dot(a, b, (0, 0), precision)


def split2(x):
    hi = x.astype(BF16)
    return hi, (x - hi.astype(F32)).astype(BF16)


def split3(x, axis):
    hi, rest = x.astype(BF16), x - x.astype(BF16).astype(F32)
    mid = rest.astype(BF16)
    return jnp.concatenate([hi, mid, (rest - mid.astype(F32)).astype(BF16)], axis=axis)


def tn2(a, b):
    both = tn(a, jnp.concatenate(split2(b), axis=1))
    return both[:, : b.shape[1]] + both[:, b.shape[1] :]


def nt2(a, b):
    both = nt(a, jnp.concatenate(split2(b), axis=0))
    return both[:, : b.shape[0]] + both[:, b.shape[0] :]


def matrix(m):
    return pl.ds(m * HEAD_DIM, HEAD_DIM)


def tail_of(ref):
    return pl.ds(ref.shape[-2] - TAIL, TAIL)


def extra(m):
    return pl.ds(2 * HEAD_DIM + m * EXTRA, EXTRA)


def extra_in(m):
    return pl.ds(4 * HEAD_DIM + m * EXTRA, EXTRA)


def iota(shape, dim):
    return lax.broadcasted_iota(jnp.int32, shape, dim)


def whole16(x):
    return x.astype(jnp.int32).astype(I16)


def wide(x):
    return x.astype(jnp.int32).astype(F32)


def encode(x):
    top = jnp.maximum(jnp.max(jnp.abs(x), axis=0, keepdims=True), 1e-30)
    power = jnp.ceil(jnp.log2(top) * 8.0)
    return jnp.clip(jnp.floor(x * jnp.exp2(15.0 - power / 8.0) + 0.5), -32767.0, 32767.0), power


def decode(steps, power):
    return wide(steps) * jnp.exp2(power / 8.0 - 15.0)


def encode18(x):
    top = jnp.maximum(jnp.max(jnp.abs(x), axis=0, keepdims=True), 1e-30)
    power = jnp.ceil(jnp.log2(top) * 8.0)
    steps = jnp.clip(jnp.floor(x * jnp.exp2(17.0 - power / 8.0) + 0.5), -131071.0, 131071.0)
    high = jnp.floor(steps * 0.25)
    low = steps - 4.0 * high
    return high, sum(low[k * EXTRA : (k + 1) * EXTRA] * 4.0**k for k in range(8)) - 32768.0, power


def decode18(high, packed, power):
    packed = wide(packed) + 32768.0
    digits = [jnp.floor(packed * 0.25**k) for k in range(8)]
    low = jnp.concatenate(
        [d - 4.0 * above for d, above in zip(digits, digits[1:] + [jnp.zeros_like(packed)])], axis=0
    )
    return (wide(high) * 4.0 + low) * jnp.exp2(power / 8.0 - 17.0)


def encode2(x):
    power = jnp.ceil(jnp.log2(jnp.maximum(jnp.abs(x), 1e-30)))
    scaled = x * jnp.exp2(14.0 - power)
    high = jnp.floor(scaled + 0.5)
    return power, high, jnp.floor((scaled - high) * 16384.0 + 0.5)


def decode2(power, high, low):
    return (high + low / 16384.0) * jnp.exp2(power - 14.0)


def log_parts(log):
    coarse = jnp.floor(log * 256.0 + 0.5)
    return coarse, jnp.floor((log - coarse / 256.0) * 8388608.0 + 0.5)


def log_whole(coarse, fine):
    return coarse / 256.0 + fine / 8388608.0


def rows16(*rows):
    at = iota((TAIL, LANES), 0)
    total = jnp.zeros((TAIL, LANES), F32)
    for i, row in enumerate(rows):
        total = jnp.where(at == i, row, total)
    return whole16(total)


def doc_of(pos, offsets_ref):
    total = (pos >= offsets_ref[0, 0]).astype(jnp.int32)
    for i in range(1, DOCS):
        total = total + (pos >= offsets_ref[0, i]).astype(jnp.int32)
    return total


def place():
    return lax.axis_index("seg") * lax.axis_size("grp") + lax.axis_index("grp")


def decays(gates, bias, offsets_ref):
    heads, length = gates.shape
    first = place() * length
    same = iota((heads, heads), 0) == iota((heads, heads), 1)
    logits = gates.astype(F32) + jnp.sum(jnp.where(same, bias, 0.0), axis=1, keepdims=True)
    step = -(jnp.maximum(logits, 0.0) + jnp.log1p(jnp.exp(-jnp.abs(logits))))
    causal = iota((length, length), 0) >= iota((length, length), 1)
    terms = nt(causal.astype(BF16), split3(step, 0))
    cumulative = terms[:, :heads] + (terms[:, heads : 2 * heads] + terms[:, 2 * heads :])
    doc = doc_of(first + iota((length, 1), 0), offsets_ref)
    doc_last = doc_of(first + length - 1, offsets_ref)
    before = jnp.where(first > 0, doc_of(first - 1, offsets_ref), -1)
    entry = jnp.exp(cumulative) * (doc == before).astype(F32)
    tail = jnp.exp(cumulative[length - 1 :, :] - cumulative) * (doc == doc_last).astype(F32)
    return first, logits, step, causal, cumulative, doc, entry, tail, doc_last == before


def fetch(refs, held, sems):
    parts = sems.shape[1]
    width = held.shape[2] // parts
    copies = [
        [
            pltpu.make_async_copy(
                ref.at[0, :, pl.ds(p * width, width)], held.at[i, :, pl.ds(p * width, width)], sems.at[i, p]
            )
            for i, ref in enumerate(refs)
        ]
        for p in range(parts)
    ]
    for group in copies:
        for copy in group:
            copy.start()
    return copies


def arrive(copies, head, heads):
    each = heads // len(copies)
    if head % each == 0:
        for copy in copies[head // each]:
            copy.wait()


def states_kernel(
    query_ref, key_ref, value_ref, dout_ref, gate_ref, bias_ref, offsets_ref,
    pay_ref, held, sems, gate_held, bias_held, offsets_held, small_sems, pay, pay_sems,
):
    heads = bias_ref.shape[1]
    small = [
        pltpu.make_async_copy(gate_ref.at[0], gate_held, small_sems.at[0]),
        pltpu.make_async_copy(bias_ref, bias_held, small_sems.at[1]),
        pltpu.make_async_copy(offsets_ref, offsets_held, small_sems.at[2]),
    ]
    for copy in small:
        copy.start()
    copies = fetch((query_ref, key_ref, value_ref, dout_ref), held, sems)
    for copy in small:
        copy.wait()
    _, _, _, _, cumulative, _, entry, tail, passes = decays(gate_held[...], bias_held[...], offsets_held)
    coarse, fine = log_parts(jnp.where(passes, jnp.maximum(cumulative[-1:, :], -120.0), -128.0))
    powers, sent = {}, []
    for h in range(heads):
        arrive(copies, h, heads)
        cols = matrix(h)
        one = slice(h, h + 1)
        slot, m = divmod(h, 2)
        for at, left, right, weight in ((m, 1, 2, tail[:, one]), (2 + m, 0, 3, entry[:, one] * SCALE)):
            own = tn2(held[left, :, cols], held[right, :, cols].astype(F32) * weight)
            high, low, powers[at] = encode18(own)
            pay[slot, matrix(at), :] = whole16(high)
            pay[slot, extra_in(at), :] = whole16(low)
        if m == 1:
            pay[slot, tail_of(pay), :] = rows16(
                *(powers[i] for i in range(4)),
                *(x[:, i : i + 1] for i in (h - 1, h) for x in (coarse, fine)),
            )
            sent.append(pltpu.make_async_copy(pay.at[slot], pay_ref.at[slot], pay_sems.at[slot]))
            sent[-1].start()
    for copy in sent:
        copy.wait()


def chunk_logs(tails, m):
    return [log_whole(t[4 + 2 * m : 5 + 2 * m], t[5 + 2 * m : 6 + 2 * m]) for t in tails]


def totals_kernel(pay_ref, _, own_ref, *send_refs):
    count = pay_ref.shape[0]
    tails = [wide(pay_ref[c, tail_of(pay_ref), :]) for c in range(count)]
    mine, segments = lax.axis_index("seg"), lax.axis_size("seg")
    powers, logs = [], []
    for m in range(2):
        log = chunk_logs(tails, m)
        logs.extend(log_parts(jnp.maximum(sum(log), -128.0)))
        ends = []
        for where, order in ((m, range(count)), (2 + m, range(count - 1, -1, -1))):
            carry = jnp.zeros((HEAD_DIM, HEAD_DIM), F32)
            for c in order:
                own = decode18(
                    pay_ref[c, matrix(where), :], pay_ref[c, extra_in(where), :], tails[c][where : where + 1]
                )
                own_ref[c, matrix(where), :] = own
                carry = jnp.exp(log[c]) * carry + own
            ends.append(encode18(carry))
        powers.append([end[2] for end in ends])
        for distance, send_ref in enumerate(send_refs, 1):
            later = mine + distance < segments
            send_ref[matrix(m), :] = whole16(jnp.where(later, ends[0][0], ends[1][0]))
            send_ref[extra(m), :] = whole16(jnp.where(later, ends[0][1], ends[1][1]))
    for distance, send_ref in enumerate(send_refs, 1):
        later = mine + distance < segments
        send_ref[tail_of(send_ref), :] = rows16(*(jnp.where(later, *pair) for pair in powers), *logs)


def scan_kernel(pay_ref, own_ref, *refs):
    *got_refs, out_ref, held = refs
    count = pay_ref.shape[0]
    mine = lax.axis_index("seg")
    tails = [wide(pay_ref[c, tail_of(pay_ref), :]) for c in range(count)]
    got_tails = [wide(ref[tail_of(ref), :]) for ref in got_refs]
    at = iota((2 * count, LANES), 0)
    flows = jnp.zeros((2 * count, LANES), F32)
    powers = [[None] * 4 for _ in range(count)]
    for m in range(2):
        log = chunk_logs(tails, m)
        sent = [
            (
                jnp.exp(log_whole(t[2 + 2 * m : 3 + 2 * m], t[3 + 2 * m : 4 + 2 * m])),
                decode18(ref[matrix(m), :], ref[extra(m), :], t[m : m + 1]),
            )
            for ref, t in zip(got_refs, got_tails)
        ]
        state = jnp.zeros((HEAD_DIM, HEAD_DIM), F32)
        for d in range(len(sent), 0, -1):
            state = jnp.where(mine >= d, sent[d - 1][0] * state + sent[d - 1][1], state)
        grad = jnp.zeros((HEAD_DIM, HEAD_DIM), F32)
        for d in range(1, len(sent) + 1):
            grad = jnp.where(mine < d, sent[d - 1][0] * grad + sent[d - 1][1], grad)
        for where, carry, order in ((m, state, range(count)), (2 + m, grad, range(count - 1, -1, -1))):
            for i, c in enumerate(order):
                steps, powers[c][where] = encode(carry)
                out_ref[c, matrix(where), :] = whole16(steps)
                passing = jnp.exp(log[c])
                if where == m:
                    held[c] = carry
                else:
                    flow = passing * jnp.sum(held[c] * carry, axis=0, keepdims=True)
                    flows = jnp.where(at == 2 * c + m, flow, flows)
                if i < count - 1:
                    carry = passing * carry + own_ref[c, matrix(where), :]
    parts = encode2(jnp.sum(flows, axis=1, keepdims=True))
    for c in range(count):
        out_ref[c, tail_of(out_ref), :] = rows16(
            *powers[c], *(part[2 * c + m : 2 * c + m + 1] for m in range(2) for part in parts)
        )


def local_kernel(
    query_ref, key_ref, value_ref, dout_ref, gate_ref, bias_ref, offsets_ref,
    dq_ref, dk_ref, dv_ref, rows_ref, cols_ref, held, sems,
):
    heads, length = gate_ref.shape[1:]
    copies = fetch((query_ref, key_ref, value_ref, dout_ref), held, sems)
    first, logits, step, causal, cumulative, doc, entry, tail, passes = decays(
        gate_ref[0], bias_ref[...], offsets_ref
    )
    cumulative_row = nt(step, causal.astype(F32), HIGHEST)
    linked = causal & (doc == doc_of(first + iota((1, length), 1), offsets_ref))
    lane = iota((length, heads), 1)
    sublane = iota((heads, length), 0)
    ends = jnp.zeros((length, heads), F32)
    ends_row = jnp.zeros((heads, length), F32)
    for h in range(heads):
        arrive(copies, h, heads)
        cols = matrix(h)
        q, k, v, d = (held[i, :, cols] for i in range(4))
        weights = jnp.where(
            linked,
            jnp.exp(jnp.where(linked, cumulative[:, h : h + 1] - cumulative_row[h : h + 1, :], 0.0)),
            0.0,
        ) * SCALE
        probs = nt(q, k) * weights
        dprobs = nt(d, v)
        pairs = probs * dprobs
        probs = probs.astype(BF16)
        dscores = (dprobs * weights).astype(BF16)
        dq_ref[:, cols] = nn(dscores, k)
        dk_ref[:, cols] = tn(dscores, q)
        dv_ref[:, cols] = tn(probs, d)
        ends = jnp.where(lane == h, jnp.sum(pairs, axis=1, keepdims=True), ends)
        ends_row = jnp.where(sublane == h, jnp.sum(pairs, axis=0, keepdims=True), ends_row)
    causal = causal.astype(F32)
    rows_ref[0] = tn(ends, causal, HIGHEST) - nn(ends_row, causal, HIGHEST)
    rows_ref[1] = -1.0 / (1.0 + jnp.exp(-logits))
    cols_ref[0] = entry * SCALE
    cols_ref[1] = tail


def received(state_ref, head):
    slot, m = divmod(head, 2)
    tail = wide(state_ref[slot, tail_of(state_ref), :])
    pair = tuple(decode(state_ref[slot, matrix(i), :], tail[i : i + 1]) for i in (m, 2 + m))
    return *pair, decode2(*(tail[i : i + 1, :1] for i in range(4 + 3 * m, 7 + 3 * m)))


def gates_kernel(
    query_ref, key_ref, value_ref, dout_ref, rows_ref, cols_ref, state_ref, dgate_ref, dbias_ref
):
    heads, length = dgate_ref.shape[1:]
    lane = iota((length, heads), 1)
    sublane = iota((heads, 1), 0)
    ends = jnp.zeros((length, heads), F32)
    starts = jnp.zeros((length, heads), F32)
    flows = jnp.zeros((heads, 1), F32)
    for h in range(heads):
        state32, grad32, flow = received(state_ref, h)
        q, k, v, d = (ref[0, :, matrix(h)] for ref in (query_ref, key_ref, value_ref, dout_ref))
        at_end = jnp.sum(q.astype(F32) * nt2(d, state32), axis=1, keepdims=True)
        at_start = jnp.sum(k.astype(F32) * nt2(v, grad32), axis=1, keepdims=True)
        ends = jnp.where(lane == h, at_end, ends)
        starts = jnp.where(lane == h, at_start, starts)
        flows = jnp.where(sublane == h, flow, flows)
    behind = iota((length, length), 0) - iota((length, length), 1)
    masks = jnp.concatenate([(behind >= 0).astype(BF16), (behind < 0).astype(BF16)], axis=0)
    sums = jnp.concatenate([ends * cols_ref[0], starts * cols_ref[1]], axis=0)
    terms = tn(split3(sums, 1), masks)
    terms = terms[:heads] + (terms[heads : 2 * heads] + terms[2 * heads :])
    dstep = rows_ref[0] + terms + flows
    dlogit = dstep * rows_ref[1]
    dgate_ref[0] = dlogit.astype(BF16)
    same = iota((heads, heads), 0) == iota((heads, heads), 1)
    total = jnp.sum(jnp.where(same, jnp.sum(dlogit, axis=1, keepdims=True), 0.0), axis=0, keepdims=True)
    dbias_ref[...] = jnp.broadcast_to(total[None], dbias_ref.shape)


def output_kernel(
    key_ref, value_ref, dout_ref, cols_ref, state_ref, dq_near_ref, dk_near_ref, dv_near_ref,
    dq_ref, dk_ref, dv_ref,
):
    for h in range(cols_ref.shape[2]):
        cols = matrix(h)
        entry, tail = (cols_ref[i, :, h : h + 1] for i in range(2))
        state, grad = (x.astype(BF16) for x in received(state_ref, h)[:2])
        for near_ref, out_ref, far, decay in (
            (dq_near_ref, dq_ref, nt(dout_ref[0, :, cols], state), entry),
            (dk_near_ref, dk_ref, nt(value_ref[0, :, cols], grad), tail),
            (dv_near_ref, dv_ref, nn(key_ref[0, :, cols], grad), tail),
        ):
            out_ref[0, :, cols] = (near_ref[:, cols] + decay * far).astype(BF16)


def call(kernel, out_shape, in_specs, **more):
    more.setdefault("out_specs", (VMEM,) * len(out_shape) if isinstance(out_shape, tuple) else VMEM)
    return pl.pallas_call(
        kernel, out_shape=out_shape, in_specs=in_specs, compiler_params=PARAMS, **more
    )


def shards(query, key, value, dout, gate_in, gate_bias, offsets):
    heads = gate_bias.shape[0]
    length, width = query.shape[1:]
    count, segments = lax.axis_size("grp"), lax.axis_size("seg")
    gates = jnp.swapaxes(gate_in, 1, 2)
    small = (gates, gate_bias.reshape(1, heads), offsets)
    pin = lambda xs: tuple(pltpu.with_memory_space_constraint(x, pltpu.HBM) for x in xs)
    big = pin((query, key, value, dout))
    scratch = [pltpu.VMEM((4, length, width), BF16), pltpu.SemaphoreType.DMA((4, 8))]
    packed = jax.ShapeDtypeStruct((count, 4 * HEAD_DIM + TAIL, LANES), I16)
    packed_in = jax.ShapeDtypeStruct((count, 4 * (HEAD_DIM + EXTRA) + TAIL, LANES), I16)
    pay = call(
        states_kernel,
        packed_in,
        [HBM] * 7,
        scratch_shapes=scratch
        + [
            pltpu.VMEM((heads, length), BF16),
            pltpu.VMEM((1, heads), F32),
            pltpu.SMEM(offsets.shape, jnp.int32),
            pltpu.SemaphoreType.DMA((3,)),
            pltpu.VMEM(packed_in.shape, I16),
            pltpu.SemaphoreType.DMA((count,)),
        ],
        out_specs=HBM,
    )(*big, *pin(small))
    pay = lax.all_to_all(pay, "grp", split_axis=0, concat_axis=0, tiled=True)
    near_like = jax.ShapeDtypeStruct((length, width), F32)
    *near, rows, cols = call(
        local_kernel,
        (near_like,) * 3
        + (jax.ShapeDtypeStruct((2, heads, length), F32), jax.ShapeDtypeStruct((2, length, heads), F32)),
        [HBM] * 4 + [VMEM] * 2 + [SMEM],
        scratch_shapes=scratch,
    )(*big, *small)
    total = jax.ShapeDtypeStruct((2 * HEAD_DIM + 2 * EXTRA + TAIL, LANES), I16)
    own, *sends = call(
        totals_kernel,
        (jax.ShapeDtypeStruct((count, 4 * HEAD_DIM, LANES), F32),) + (total,) * (segments - 1),
        [VMEM, pl.BlockSpec(memory_space=pl.ANY)],
    )(pay, rows)
    got = {
        d: lax.ppermute(sends[d - 1], "seg", [(i, (i + d) % segments) for i in range(segments)])
        for d in sorted(range(1, segments), key=lambda d: -min(d, segments - d))
    }
    got = [got[d] for d in range(1, segments)]
    carried = call(
        scan_kernel,
        packed,
        [VMEM] * (segments + 1),
        scratch_shapes=[pltpu.VMEM((count, HEAD_DIM, LANES), F32)],
    )(pay, own, *got)
    carried = lax.all_to_all(carried, "grp", split_axis=0, concat_axis=0, tiled=True)
    dgate, dbias = call(
        gates_kernel,
        (
            jax.ShapeDtypeStruct(gates.shape, BF16),
            jax.ShapeDtypeStruct((lax.axis_size(ALL), 1, heads), F32),
        ),
        [VMEM] * 7,
    )(query, key, value, dout, rows, cols, carried)
    everywhere = lax.all_to_all(dbias, ALL, split_axis=0, concat_axis=0, tiled=True)
    like = jax.ShapeDtypeStruct(query.shape, BF16)
    dq, dk, dv = call(output_kernel, (like,) * 3, [VMEM] * 8)(key, value, dout, cols, carried, *near)
    return dq, dk, dv, jnp.swapaxes(dgate, 1, 2), jnp.sum(everywhere, axis=(0, 1))


def solution(mesh):
    rows = P("dp", LINE, None)
    return jax.shard_map(
        shards,
        mesh=mesh,
        in_specs=(rows, rows, rows, rows, rows, P(), P("dp", None)),
        out_specs=(rows, rows, rows, rows, P()),
        check_vma=False,
    )
```
